512 devices in a mesh: cannon: 128 (over z_hi, x, y), rep: 4 (over z_lo, core).
Axes of the slice: x: 4, y: 8, z: 8 (z_hi: 4, z_lo: 2; z = z_hi * 2 + z_lo), core: 2. Of those that a mesh axis runs over, the one named last changes fastest.
Arguments:
- root_margin: bfloat16 [512, 8, 128, 128], P('cannon', 'rep'), may hold values from -2.5 to 2.5
- inverse_root: bfloat16 [512, 8, 128, 128], P('cannon', 'rep'), may hold values from -2.5 to 2.5
- hamiltonian: bfloat16 [512, 8, 128, 128], P('cannon', 'rep'), may hold values from -0.25 to 0.25
- margin_mask: int32 [512, 8], P('cannon', 'rep'), may hold values from 0 to 1, as said below
- hamilton_mask: int32 [512, 8], P('cannon', 'rep'), may hold values from 0 to 1, as said below
Outputs:
- root_next: bfloat16 [512, 8, 128, 128], P('cannon', 'rep')
- inverse_next: bfloat16 [512, 8, 128, 128], P('cannon', 'rep')
- lowdin_product: bfloat16 [512, 8, 128, 128], P('cannon', 'rep')
The draws below stay inside these ranges and needn't reach their ends.
Inputs may be any that keep to these rules, and one draw needn't show every extreme that they name: `margin_mask`: 0 or 1; slot 8 // 2 (the diagonal block) is 1 in every block row; all block rows of one index of cannon share a fill level drawn from the seed, from one eighth to full. `hamilton_mask`: 0 or 1; slot 8 // 2 (the diagonal block) is 1 in every block row; all block rows of one index of cannon share a fill level drawn from the seed, from one eighth to full.
All inputs are finite; a program needn't handle non-finite values.
Results may differ from the reference program's by a relative error of at most 0.018.
Values may be sent and summed in bfloat16 or wider, within the bound.
A program may use at most 64 MiB of HBM per device.

```python
import jax
import jax.numpy as jnp
from jax import lax

BLK = 128
NS = 8
BR_DEV = 4
NB = 512
N_REP = 4


def pattern_draw(key):
    panels = NB // BR_DEV
    fill_level = jax.random.randint(jax.random.fold_in(key, 11), (panels, 1), 1, 9)
    fill_level = jnp.repeat(fill_level, BR_DEV, axis=0)
    random_picks = jax.random.randint(jax.random.fold_in(key, 12), (NB, NS), 0, 8)
    pattern = (random_picks < fill_level).astype(jnp.int32)
    diagonal = (jnp.arange(NS) == NS // 2)[None, :]
    return jnp.where(diagonal, 1, pattern).astype(jnp.int32)


def draw_margin_mask(key, part):
    return pattern_draw(jax.random.fold_in(key, 1))


def draw_hamilton_mask(key, part):
    return pattern_draw(jax.random.fold_in(key, 2))


def block_levels(rng, extent, pieces, least, largest):
    factor_of, own = 1.0, jax.random.fold_in(rng, 6)
    for dim, parts in pieces:
        heights = jnp.exp(jax.random.uniform(jax.random.fold_in(own, dim), (parts,), jnp.float32, least / len(pieces), largest / len(pieces)))
        factor_of = factor_of * jnp.repeat(heights, extent[dim] // parts).reshape([-1 if axis == dim else 1 for axis in range(len(extent))])
    return factor_of


def centred(key, extent, deviation, bound, cuts=(), kind=jnp.bfloat16):
    result = deviation * jax.random.normal(key, extent, jnp.float32)
    if cuts:
        result = result * block_levels(key, extent, cuts, -0.22, 0.18)
    return jnp.clip(result, -bound, bound).astype(kind)


def setup_inputs(seed: int = 0) -> dict:
    streams_of = jax.random.split(jax.random.key(seed), 6)
    root_margin = centred(streams_of[0], (NB, NS, BLK, BLK), ((BLK * NS) ** -0.25), 2.5, ((0, 128), (1, 4)))
    inverse_root = centred(streams_of[1], (NB, NS, BLK, BLK), ((BLK * NS) ** -0.25), 2.5, ((0, 128), (1, 4)))
    hamiltonian = centred(streams_of[2], (NB, NS, BLK, BLK), (0.6 / (BLK * NS) ** 0.5), 0.25, ((0, 128), (1, 4)))
    margin_mask = draw_margin_mask(jax.random.fold_in(streams_of[5], 71), 0)
    hamilton_mask = draw_hamilton_mask(jax.random.fold_in(streams_of[5], 71), 0)
    return dict(root_margin=root_margin, inverse_root=inverse_root, hamiltonian=hamiltonian, margin_mask=margin_mask, hamilton_mask=hamilton_mask)


def band_product(first_factor, second_factor, pattern):
    slot_count = first_factor.shape[1]
    half_band = slot_count // 2
    group_slots = slot_count // N_REP
    summed = jnp.zeros(first_factor.shape, jnp.float32)
    for replica in range(N_REP):
        partial_value = jnp.zeros(first_factor.shape, jnp.float32)
        for offset in range(replica * group_slots, (replica + 1) * group_slots):
            shifted = jnp.roll(second_factor, half_band - offset, axis=0)
            first_slot = max(0, offset - half_band)
            last_slot = min(slot_count, offset + half_band)
            addend = jnp.einsum("ipq,itqr->itpr", first_factor[:, offset].astype(jnp.float32),
                                shifted[:, first_slot - offset + half_band:last_slot - offset + half_band].astype(jnp.float32))
            partial_value = partial_value.at[:, first_slot:last_slot].add(addend)
        summed = summed + lax.optimization_barrier(partial_value.astype(jnp.bfloat16)).astype(jnp.float32)
    return summed * pattern[:, :, None, None].astype(jnp.float32)


def reference(root_margin, inverse_root, hamiltonian, margin_mask, hamilton_mask):
    margin_scale = margin_mask[:, :, None, None].astype(jnp.bfloat16)
    hamilton_scale = hamilton_mask[:, :, None, None].astype(jnp.bfloat16)
    root_masked = root_margin * margin_scale
    inverse_masked = inverse_root * margin_scale
    hamilton_masked = hamiltonian * hamilton_scale
    product = band_product(inverse_masked, root_masked, margin_mask)
    slot_ids = jnp.arange(NS)
    diagonal = (slot_ids == NS // 2).astype(jnp.float32)[None, :, None, None] * jnp.eye(BLK, dtype=jnp.float32)[None, None]
    polynomial = (1.5 * diagonal - 0.5 * product).astype(jnp.bfloat16)
    inverse_next = band_product(polynomial, inverse_masked, margin_mask).astype(jnp.bfloat16)
    root_next = band_product(root_masked, polynomial, margin_mask).astype(jnp.bfloat16)
    lowdin_product = band_product(inverse_next, hamilton_masked, hamilton_mask).astype(jnp.bfloat16)
    return root_next, inverse_next, lowdin_product
```

```python
import jax
import jax.numpy as jnp
from jax import lax
from jax.experimental import pallas as pl
from jax.experimental.pallas import tpu as pltpu
from jax.sharding import PartitionSpec as P

MESH = pl.DeviceIdType.MESH
BLK = 128
NS = 8
HALF = 4
ROWS = 4
Z_PANELS = 32
SPAN = ROWS + NS - 1


def rect(j, slots):
    return (j + HALF, j + min(slots), len(slots)) if slots else None


def slots_of(role):
    return (2 * role, 2 * role + 1)


def pick(role, allowed):
    return [u for u in slots_of(role) if u in allowed]


def need_up(j):
    return range(HALF - j, NS)


def need_down(j):
    return range(0, NS - 1 - j) if j < 3 else ()


def shift(area, link):
    move = {"p": -ROWS, "P": -ROWS, "m": ROWS, "M": ROWS}.get(link, 0)
    return (area[0] + move, area[1] + move, area[2])


EVERY = (0, 1, 2, 3)
FLIP = {"c": 1, "z": 2, "p": 0, "m": 0, "P": 2, "M": 2}
PLAIN, LAST, FIRST = 0, 1, 2
KINDS = (PLAIN, LAST, FIRST)
ENDS = {
    (None, False): (KINDS, KINDS),
    ("p", False): ((PLAIN, FIRST), (PLAIN, LAST)),
    ("p", True): ((LAST,), (FIRST,)),
    ("m", False): ((PLAIN, LAST), (PLAIN, FIRST)),
    ("m", True): ((FIRST,), (LAST,)),
}


class Message:
    def __init__(self, array, link, areas, index, senders, receivers):
        self.array, self.link, self.areas, self.index = array, link, areas, index
        self.senders, self.receivers = senders, receivers


class Table:
    def __init__(self):
        self.rows = {}

    def put(self, name, array, link, areas, senders, receivers):
        areas = {role: area for role, area in areas.items() if area is not None}
        if areas:
            self.rows[name] = Message(array, link, areas, len(self.rows), senders, receivers)

    def add(self, name, link, areas, far=False):
        way = link.lower() if link in "pPmM" else None
        self.put(name, name[0], link, areas, *ENDS[way, far])

    def relay(self, name, link, of, roles=EVERY, keep=None):
        row = self.rows.get(of)
        if row is None:
            return
        got = {}
        for role in roles:
            sender = role ^ FLIP[row.link]
            if sender in row.areas:
                area = shift(row.areas[sender], row.link)
                got[role] = area if keep is None else keep(area)
        senders = row.receivers
        receivers = senders
        if link in "pm":
            ends = ENDS[link, False]
            senders, receivers = tuple(k for k in ends[0] if k in senders), ends[1]
        self.put(name, name[0], link, got, senders, receivers)


def within(area, row, low, high):
    first, end = max(area[1], low), min(area[1] + area[2], high)
    return (area[0], first, end - first) if end > first else None


def build_table():
    t = Table()
    for j in range(ROWS):
        low, high = range(HALF - j, HALF), range(HALF, NS - 1 - j)
        up, down = need_up(j), need_down(j)
        own = {r: rect(j, slots_of(r)) for r in EVERY}

        def some(allowed, roles=EVERY, other=0):
            return {r: rect(j, pick(r ^ other, allowed)) for r in roles}

        for a in "RI":
            t.add((a, "zo", j), "z", own)
            t.add((a, "co", j), "c", own)
            t.relay((a, "cz", j), "c", (a, "zo", j))
            t.add((a, "po", j), "p", some(up))
            t.add((a, "mo", j), "m", some(down))
            t.add((a, "mz", j), "m", some(down, EVERY, 2))
            t.relay((a, "cpo", j), "c", (a, "po", j))
            t.relay((a, "cmo", j), "c", (a, "mo", j))
            t.relay((a, "cmz", j), "c", (a, "mz", j))
        t.add(("R", "pz", j), "p", some(up, EVERY, 2))
        t.relay(("R", "cpz", j), "c", ("R", "pz", j))
        t.relay(("I", "zpo", j), "z", ("I", "po", j))
        t.relay(("I", "czpo", j), "c", ("I", "zpo", j))
        for a, plus, minus in (("R", "P", "M"), ("I", "p", "m")):
            t.add((a, "Xpo", j), plus, some(up, (2, 3)), True)
            t.add((a, "Xpz", j), plus, some(up, (2, 3), 2), True)
            t.add((a, "Xmo", j), minus, some(down, (0, 1)), True)
            t.add((a, "Xmz", j), minus, some(down, (0, 1), 2), True)
            for end in ("po", "pz", "mo", "mz"):
                t.relay((a, "Xc" + end, j), "c", (a, "X" + end, j))
                t.relay((a, "Xz" + end, j), "z", (a, "X" + end, j))
                t.relay((a, "Xcz" + end, j), "c", (a, "Xz" + end, j))

        t.add(("H", "co", j), "c", own)
        t.add(("H", "zo", j), "z", {r: rect(j, pick(r, low if r < 2 else high)) for r in EVERY})
        t.relay(("H", "cz", j), "c", ("H", "zo", j))
        t.relay(("H", "pz", j), "p", ("H", "zo", j), (0, 1))
        t.relay(("H", "cpz", j), "c", ("H", "pz", j))
        beyond = range(NS - 1 - j, NS)
        t.add(("H", "po", j), "p", {r: rect(j, pick(r, low if r < 2 else beyond)) for r in EVERY})
        t.relay(("H", "cpo", j), "c", ("H", "po", j))
        t.relay(("H", "zpo", j), "z", ("H", "po", j), (2, 3))
        t.relay(("H", "czpo", j), "c", ("H", "zpo", j))
        t.add(("H", "Xpo", j), "P", some(up, (2, 3)), True)
        t.add(("H", "Xpz", j), "P", some(low, (2, 3), 2), True)
        t.relay(("H", "Xcpo", j), "c", ("H", "Xpo", j))
        t.relay(("H", "Xcpz", j), "c", ("H", "Xpz", j))
        t.relay(("H", "Xzpo", j), "z", ("H", "Xpo", j), EVERY, lambda area: within(area, j, HALF, SPAN))
        t.relay(("H", "Xczpo", j), "c", ("H", "Xzpo", j))
        if j < 3:
            t.add(("H", "mo", j), "m", {r: rect(j, pick(r, range(HALF) if r < 2 else high)) for r in EVERY})
            t.relay(("H", "cmo", j), "c", ("H", "mo", j))
            t.relay(("H", "zmo", j), "z", ("H", "mo", j), (0, 1), lambda area: within(area, j, area[0] - HALF + 1, SPAN))
            t.relay(("H", "czmo", j), "c", ("H", "zmo", j))
            t.add(("H", "Xmo", j), "M", some(range(1, HALF), (0, 1)), True)
            t.add(("H", "Xmz", j), "M", some(high, (0, 1), 2), True)
            t.add(("H", "Xml", j), "m", some(range(0, 3 - j), (0, 1)), True)
            for end in ("mo", "mz", "ml"):
                t.relay(("H", "Xc" + end, j), "c", ("H", "X" + end, j))

        core = 0 if j in (0, 3) else 1
        wide, few = rect(j, up), rect(j, range(NS - j, NS))
        t.add(("P", "p", j), "p", {core: wide, 2 + core: few})
        t.relay(("P", "cp", j), "c", ("P", "p", j))
        t.add(("P", "Xp", j), "P", {2 + core: wide}, True)
        t.add(("P", "Xq", j), "p", {2 + core: few}, True)
        if j < 3:
            few, wide = rect(j, range(0, 3 - j)), rect(j, range(1, NS - 1 - j))
            t.add(("P", "m", j), "m", {core: few, 2 + core: wide})
            t.relay(("P", "cm", j), "c", ("P", "m", j))
            t.add(("P", "Xm", j), "M", {core: wide}, True)
            t.add(("P", "Xn", j), "m", {core: few}, True)
        for end in ("p", "q", "m", "n"):
            t.relay(("P", "Xc" + end, j), "c", ("P", "X" + end, j))
    for name, link in (("zo", "z"), ("co", "c"), ("cz", "c")):
        t.add(("M", name, 0), link, {r: (r ^ 2 if name == "cz" else r, 0, 1) for r in EVERY})
    return t


TABLE = build_table()


def view(refs, array, area):
    row, col, wide = area
    if array == "M":
        return refs["M"].at[pl.ds(row * 8, 8), :]
    return refs[array].at[pl.ds(row * BLK, BLK), pl.ds(col * BLK, wide * BLK)]


class Role:
    def __init__(self, kind, role, refs, send_sem, recv_sem, cannon, panels):
        self.kind, self.role, self.refs = kind, role, refs
        self.send_sem, self.recv_sem = send_sem, recv_sem
        self.cannon, self.panels = cannon, panels

    def copy(self, row, sender):
        area = row.areas[sender]
        panel = self.cannon
        if row.link in "pP":
            panel = lax.rem(self.cannon + 1, self.panels)
        if row.link in "mM":
            panel = lax.rem(self.cannon + self.panels - 1, self.panels)
        return pltpu.make_async_remote_copy(
            src_ref=view(self.refs, row.array, area),
            dst_ref=view(self.refs, row.array, shift(area, row.link)),
            send_sem=self.send_sem.at[row.index],
            recv_sem=self.recv_sem.at[row.index],
            device_id=(panel, self.role ^ FLIP[row.link]),
            device_id_type=MESH,
        )

    def send_one(self, name):
        row = TABLE.rows.get(name)
        if row is not None and self.kind in row.senders and self.role in row.areas:
            self.copy(row, self.role).start()

    def recv_one(self, name):
        row = TABLE.rows.get(name)
        if row is None or self.kind not in row.receivers:
            return False
        sender = self.role ^ FLIP[row.link]
        if sender not in row.areas:
            return False
        self.copy(row, sender).wait_recv()
        return True

    def send(self, array, *ends):
        for j in range(ROWS):
            for end in ends:
                self.send_one((array, end, j))

    def recv(self, array, *ends):
        for j in range(ROWS):
            for end in ends:
                self.recv_one((array, end, j))

    def pass_on(self, array, end, *onward):
        for j in range(ROWS):
            if self.recv_one((array, end, j)):
                for then in onward:
                    self.send_one((array, then, j))

    def drain(self):
        for row in TABLE.rows.values():
            if self.kind in row.senders and self.role in row.areas:
                self.copy(row, self.role).wait_send()


def kernel(panels, root_in, inverse_in, hamilton_in, margin_in, hamilton_mask_in,
           root_out, inverse_out, lowdin_out,
           root, inverse, hamilton, poly, margin, next_rows, send_sem, recv_sem):
    cannon, rep = lax.axis_index("cannon"), lax.axis_index("rep")
    refs = {"R": root, "I": inverse, "H": hamilton, "P": poly, "M": margin}
    ahead, behind = lax.rem(cannon + 1, panels), lax.rem(cannon + panels - 1, panels)
    sibling, across = rep + 1 - 2 * lax.rem(rep, 2), lax.rem(rep + 2, 4)

    place = lax.rem(cannon, Z_PANELS)
    far = ((place == Z_PANELS - 1) & (rep >= 2)) | ((place == 0) & (rep < 2))
    beyond = lax.rem(cannon + jnp.where(place == 0, panels - 1, 1), panels)

    barrier = pltpu.get_barrier_semaphore()
    for peer in ((ahead, rep), (behind, rep), (cannon, sibling), (cannon, across)):
        pl.semaphore_signal(barrier, inc=1, device_id=peer, device_id_type=MESH)

    @pl.when(far)
    def _():
        pl.semaphore_signal(barrier, inc=1, device_id=(beyond, across), device_id_type=MESH)

    for array, source, scale in (
        (root, root_in, margin_in), (inverse, inverse_in, margin_in), (hamilton, hamilton_in, hamilton_mask_in),
    ):
        for j in range(ROWS):
            for b in range(2):
                keep = scale[b, j].astype(jnp.float32).astype(jnp.bfloat16)
                at = pl.multiple_of((j + 2 * rep + b) * BLK, BLK)
                array[pl.ds((j + HALF) * BLK, BLK), pl.ds(at, BLK)] = source[j, b] * keep
    for j in range(ROWS):
        for b in range(2):
            keep = margin_in[b, j].astype(jnp.float32)
            margin[pl.ds(rep * 8 + j * 2 + b, 1), :] = jnp.full((1, BLK), keep, jnp.float32)
    for array in (root, inverse, hamilton, poly):
        for row in range(SPAN):
            right = row + HALF
            if right < SPAN:
                array[row * BLK:(row + 1) * BLK, right * BLK:] = jnp.zeros((BLK, (SPAN - right) * BLK), jnp.bfloat16)
            left = row - HALF
            if left > 0:
                array[row * BLK:(row + 1) * BLK, :left * BLK] = jnp.zeros((BLK, left * BLK), jnp.bfloat16)

    @pl.when(far)
    def _():
        pl.semaphore_wait(barrier, 5)

    @pl.when(jnp.logical_not(far))
    def _():
        pl.semaphore_wait(barrier, 4)

    def by_role(plan):
        for kind in KINDS:
            here = {PLAIN: (place > 0) & (place < Z_PANELS - 1), LAST: place == Z_PANELS - 1, FIRST: place == 0}[kind]
            for role in EVERY:
                @pl.when(here & (rep == role))
                def _():
                    plan(Role(kind, role, refs, send_sem, recv_sem, cannon, panels))

    def gather(d):
        d.send("R", "zo", "co")
        d.send("R", "po", "mo", "Xpo", "Xmo")
        d.send("M", "zo", "co")
        d.send("I", "zo", "co")
        d.pass_on("R", "zo", "cz", "pz", "mz", "Xpz", "Xmz")
        d.send("I", "po", "mo", "Xpo", "Xmo")
        d.pass_on("M", "zo", "cz")
        d.pass_on("R", "po", "cpo")
        d.pass_on("R", "mo", "cmo")
        d.send("H", "zo", "co", "po", "mo", "Xpo", "Xmo", "Xml")
        d.pass_on("I", "zo", "cz", "mz", "Xmz", "Xpz")
        d.pass_on("R", "pz", "cpz")
        d.pass_on("R", "mz", "cmz")
        for end in ("po", "mo", "pz", "mz"):
            d.pass_on("R", "X" + end, "Xz" + end, "Xc" + end)
        d.pass_on("I", "po", "cpo", "zpo")
        d.pass_on("H", "zo", "cz", "pz", "Xpz", "Xmz")
        for end in ("po", "mo", "pz", "mz"):
            d.pass_on("R", "Xz" + end, "Xcz" + end)
        d.recv("M", "co", "cz")
        d.recv("I", "co", "cz")
        d.recv("R", "co", "cz", "cpo", "cpz", "cmo", "cmz")
        for end in ("po", "mo", "pz", "mz"):
            d.recv("R", "Xc" + end, "Xcz" + end)

    by_role(gather)

    def mask_row(i):
        return jnp.concatenate([margin[(t // 2) * 8 + i * 2 + t % 2:(t // 2) * 8 + i * 2 + t % 2 + 1, :]
                                for t in range(NS)], axis=1)

    def window(i):
        return slice(i * BLK, (i + NS) * BLK)

    def own(i):
        return slice((i + HALF) * BLK, (i + HALF + 1) * BLK)

    at_row = lax.broadcasted_iota(jnp.int32, (BLK, NS * BLK), 0)
    at_col = lax.broadcasted_iota(jnp.int32, (BLK, NS * BLK), 1)
    diagonal = jnp.where(at_col - HALF * BLK == at_row, 1.5, 0.0).astype(jnp.float32)
    for i in range(ROWS):
        product = jnp.dot(inverse[own(i), window(i)], root[window(i), window(i)], preferred_element_type=jnp.float32)
        poly[own(i), window(i)] = (diagonal - 0.5 * (product * mask_row(i))).astype(jnp.bfloat16)

    def exchange(d):
        d.send("P", "p", "m", "Xp", "Xq", "Xm", "Xn")
        d.pass_on("I", "mo", "cmo")
        d.pass_on("I", "mz", "cmz")
        for end in ("po", "mo", "pz", "mz"):
            d.pass_on("I", "X" + end, "Xz" + end, "Xc" + end)
        d.pass_on("I", "zpo", "czpo")
        d.pass_on("H", "po", "cpo", "zpo")
        d.pass_on("H", "mo", "cmo", "zmo")
        d.pass_on("H", "pz", "cpz")
        for end in ("po", "mo", "pz", "mz"):
            d.pass_on("I", "Xz" + end, "Xcz" + end)
        d.recv("I", "cpo", "cmo", "cmz", "czpo")
        for end in ("po", "mo", "pz", "mz"):
            d.recv("I", "Xc" + end, "Xcz" + end)

    by_role(exchange)

    for i in range(ROWS):
        product = jnp.dot(poly[own(i), window(i)], inverse[window(i), window(i)], preferred_element_type=jnp.float32)
        next_rows[i] = (product * mask_row(i)).astype(jnp.bfloat16)
        mine = next_rows[i, :, pl.ds(pl.multiple_of(2 * rep * BLK, 2 * BLK), 2 * BLK)]
        for b in range(2):
            inverse_out[i, b] = mine[:, b * BLK:(b + 1) * BLK]

    def settle(d):
        d.pass_on("H", "zpo", "czpo")
        d.pass_on("H", "zmo", "czmo")
        d.pass_on("H", "Xpo", "Xzpo", "Xcpo")
        d.pass_on("H", "Xpz", "Xcpz")
        for end in ("mo", "mz", "ml"):
            d.pass_on("H", "X" + end, "Xc" + end)
        d.pass_on("H", "Xzpo", "Xczpo")
        d.pass_on("P", "p", "cp")
        d.pass_on("P", "m", "cm")
        for end in ("q", "n", "p", "m"):
            d.pass_on("P", "X" + end, "Xc" + end)
        d.recv("H", "co", "cz", "cpo", "cpz", "cmo", "czpo", "czmo")
        d.recv("H", "Xcpo", "Xcpz", "Xczpo", "Xcmo", "Xcmz", "Xcml")

    by_role(settle)

    def narrow(first, second, i):
        cols = pl.ds(pl.multiple_of((i + 2 * rep) * BLK, BLK), 2 * BLK)
        return jnp.dot(first, second[window(i), cols], preferred_element_type=jnp.float32)

    for i in range(ROWS):
        product = narrow(next_rows[i], hamilton, i)
        for b in range(2):
            keep = hamilton_mask_in[b, i].astype(jnp.float32)
            lowdin_out[i, b] = (product[:, b * BLK:(b + 1) * BLK] * keep).astype(jnp.bfloat16)

    def last(d):
        d.recv("P", "cp", "cm", "Xcp", "Xcq", "Xcm", "Xcn")

    by_role(last)

    for i in range(ROWS):
        product = narrow(root[own(i), window(i)], poly, i)
        for b in range(2):
            keep = margin_in[b, i].astype(jnp.float32)
            root_out[i, b] = (product[:, b * BLK:(b + 1) * BLK] * keep).astype(jnp.bfloat16)

    def finish(d):
        d.drain()

    by_role(finish)


def solution(mesh):
    panels = mesh.shape["cannon"]
    count = len(TABLE.rows)
    vmem = pl.BlockSpec(memory_space=pltpu.VMEM)
    smem = pl.BlockSpec(memory_space=pltpu.SMEM)

    def body(root_margin, inverse_root, hamiltonian, margin_mask, hamilton_mask):
        shape = jax.ShapeDtypeStruct(root_margin.shape, jnp.bfloat16)

        def run(*refs):
            kernel(panels, *refs)

        band = pltpu.VMEM((SPAN * BLK, SPAN * BLK), jnp.bfloat16)
        return pl.pallas_call(
            run,
            out_shape=(shape, shape, shape),
            in_specs=[vmem, vmem, vmem, smem, smem],
            out_specs=(vmem, vmem, vmem),
            scratch_shapes=[
                band, band, band, band,
                pltpu.VMEM((4 * 8, BLK), jnp.float32),
                pltpu.VMEM((ROWS, BLK, NS * BLK), jnp.bfloat16),
                pltpu.SemaphoreType.DMA((count,)),
                pltpu.SemaphoreType.DMA((count,)),
            ],
            compiler_params=pltpu.CompilerParams(
                collective_id=0, has_side_effects=True, vmem_limit_bytes=48 << 20
            ),
            cost_estimate=pl.CostEstimate(flops=4 * 4 * 268435456, bytes_accessed=6 * 262144, transcendentals=0),
            name="newton_step",
        )(root_margin, inverse_root, hamiltonian, margin_mask.T, hamilton_mask.T)

    spec = P("cannon", "rep", None, None)
    mask = P("cannon", "rep")
    return jax.shard_map(body, mesh=mesh, in_specs=(spec, spec, spec, mask, mask),
                         out_specs=(spec, spec, spec), check_vma=False)
```

```python
import jax
import jax.numpy as jnp
from jax import lax
from jax.experimental import pallas as pl
from jax.experimental.pallas import tpu as pltpu
from jax.sharding import PartitionSpec as P

MESH = pl.DeviceIdType.MESH
BLK = 128
NS = 8
HALF = 4
ROWS = 4
Z_PANELS = 32
SPAN = ROWS + NS - 1


def rect(j, slots):
    return (j + HALF, j + min(slots), len(slots)) if slots else None


def slots_of(role):
    return (2 * role, 2 * role + 1)


def pick(role, allowed):
    return [u for u in slots_of(role) if u in allowed]


def need_up(j):
    return range(HALF - j, NS)


def need_down(j):
    return range(0, NS - 1 - j) if j < 3 else ()


def shift(area, link):
    move = {"p": -ROWS, "P": -ROWS, "m": ROWS, "M": ROWS}.get(link, 0)
    return (area[0] + move, area[1] + move, area[2])


EVERY = (0, 1, 2, 3)
FLIP = {"c": 1, "z": 2, "p": 0, "m": 0, "P": 2, "M": 2}
PLAIN, LAST, FIRST = 0, 1, 2
KINDS = (PLAIN, LAST, FIRST)
ENDS = {
    (None, False): (KINDS, KINDS),
    ("p", False): ((PLAIN, FIRST), (PLAIN, LAST)),
    ("p", True): ((LAST,), (FIRST,)),
    ("m", False): ((PLAIN, LAST), (PLAIN, FIRST)),
    ("m", True): ((FIRST,), (LAST,)),
}


class Message:
    def __init__(self, array, link, areas, index, senders, receivers):
        self.array, self.link, self.areas, self.index = array, link, areas, index
        self.senders, self.receivers = senders, receivers


class Table:
    def __init__(self):
        self.rows = {}

    def put(self, name, array, link, areas, senders, receivers):
        areas = {role: area for role, area in areas.items() if area is not None}
        if areas:
            self.rows[name] = Message(array, link, areas, len(self.rows), senders, receivers)

    def add(self, name, link, areas, far=False):
        way = link.lower() if link in "pPmM" else None
        self.put(name, name[0], link, areas, *ENDS[way, far])

    def relay(self, name, link, of, roles=EVERY, keep=None):
        row = self.rows.get(of)
        if row is None:
            return
        got = {}
        for role in roles:
            sender = role ^ FLIP[row.link]
            if sender in row.areas:
                area = shift(row.areas[sender], row.link)
                got[role] = area if keep is None else keep(area)
        senders = row.receivers
        receivers = senders
        if link in "pm":
            ends = ENDS[link, False]
            senders, receivers = tuple(k for k in ends[0] if k in senders), ends[1]
        self.put(name, name[0], link, got, senders, receivers)


def within(area, low, high):
    first, end = max(area[1], low), min(area[1] + area[2], high)
    return (area[0], first, end - first) if end > first else None


def build_table():
    t = Table()
    for j in range(ROWS):
        low, high = range(HALF - j, HALF), range(HALF, NS - 1 - j)
        up, down = need_up(j), need_down(j)
        own = {r: rect(j, slots_of(r)) for r in EVERY}

        def some(allowed, roles=EVERY, other=0):
            return {r: rect(j, pick(r ^ other, allowed)) for r in roles}

        for a in "RI":
            t.add((a, "zo", j), "z", own)
            t.add((a, "co", j), "c", own)
            t.relay((a, "cz", j), "c", (a, "zo", j))
            t.add((a, "po", j), "p", some(up))
            t.add((a, "mo", j), "m", some(down))
            t.add((a, "mz", j), "m", some(down, EVERY, 2))
            t.relay((a, "cpo", j), "c", (a, "po", j))
            t.relay((a, "cmo", j), "c", (a, "mo", j))
            t.relay((a, "cmz", j), "c", (a, "mz", j))
        t.add(("R", "pz", j), "p", some(up, EVERY, 2))
        t.relay(("R", "cpz", j), "c", ("R", "pz", j))
        t.relay(("I", "zpo", j), "z", ("I", "po", j))
        t.relay(("I", "czpo", j), "c", ("I", "zpo", j))
        for a, plus, minus in (("R", "P", "M"), ("I", "p", "m")):
            t.add((a, "Xpo", j), plus, some(up, (2, 3)), True)
            t.add((a, "Xpz", j), plus, some(up, (2, 3), 2), True)
            t.add((a, "Xmo", j), minus, some(down, (0, 1)), True)
            t.add((a, "Xmz", j), minus, some(down, (0, 1), 2), True)
            for end in ("po", "pz", "mo", "mz"):
                t.relay((a, "Xc" + end, j), "c", (a, "X" + end, j))
                t.relay((a, "Xz" + end, j), "z", (a, "X" + end, j))
                t.relay((a, "Xcz" + end, j), "c", (a, "Xz" + end, j))

        t.add(("H", "co", j), "c", own)
        t.add(("H", "zo", j), "z", {r: rect(j, pick(r, low if r < 2 else high)) for r in EVERY})
        t.relay(("H", "cz", j), "c", ("H", "zo", j))
        t.relay(("H", "pz", j), "p", ("H", "zo", j), (0, 1))
        t.relay(("H", "cpz", j), "c", ("H", "pz", j))
        beyond = range(NS - 1 - j, NS)
        t.add(("H", "po", j), "p", {r: rect(j, pick(r, low if r < 2 else beyond)) for r in EVERY})
        t.relay(("H", "cpo", j), "c", ("H", "po", j))
        t.relay(("H", "zpo", j), "z", ("H", "po", j), (2, 3))
        t.relay(("H", "czpo", j), "c", ("H", "zpo", j))
        t.add(("H", "Xpo", j), "P", some(up, (2, 3)), True)
        t.add(("H", "Xpz", j), "P", some(low, (2, 3), 2), True)
        t.relay(("H", "Xcpo", j), "c", ("H", "Xpo", j))
        t.relay(("H", "Xcpz", j), "c", ("H", "Xpz", j))
        t.relay(("H", "Xzpo", j), "z", ("H", "Xpo", j), EVERY, lambda area: within(area, HALF, SPAN))
        t.relay(("H", "Xczpo", j), "c", ("H", "Xzpo", j))
        if j < 3:
            t.add(("H", "mo", j), "m", {r: rect(j, pick(r, range(HALF) if r < 2 else high)) for r in EVERY})
            t.relay(("H", "cmo", j), "c", ("H", "mo", j))
            t.relay(("H", "zmo", j), "z", ("H", "mo", j), (0, 1), lambda area: within(area, area[0] - HALF + 1, SPAN))
            t.relay(("H", "czmo", j), "c", ("H", "zmo", j))
            t.add(("H", "Xmo", j), "M", some(range(HALF), (0, 1)), True)
            t.add(("H", "Xmz", j), "M", some(high, (0, 1), 2), True)
            t.relay(("H", "Xzmo", j), "z", ("H", "Xmo", j), EVERY, lambda area: within(area, 0, area[0] - HALF + 3 - j))
            t.relay(("H", "Xczmo", j), "c", ("H", "Xzmo", j))
            for end in ("mo", "mz"):
                t.relay(("H", "Xc" + end, j), "c", ("H", "X" + end, j))

        core = 0 if j in (0, 3) else 1
        wide, few = rect(j, up), rect(j, range(NS - j, NS))
        t.add(("P", "p", j), "p", {core: wide, 2 + core: few})
        t.relay(("P", "cp", j), "c", ("P", "p", j))
        t.add(("P", "Xp", j), "P", {2 + core: wide}, True)
        t.relay(("P", "Xq", j), "z", ("P", "Xp", j), EVERY, lambda area: within(area, HALF, SPAN))
        if j < 3:
            few, wide = rect(j, range(0, 3 - j)), rect(j, range(1, NS - 1 - j))
            t.add(("P", "m", j), "m", {core: few, 2 + core: wide})
            t.relay(("P", "cm", j), "c", ("P", "m", j))
            t.add(("P", "Xm", j), "M", {core: wide}, True)
            t.add(("P", "Xn", j), "m", {core: few}, True)
        for end in ("p", "q", "m", "n"):
            t.relay(("P", "Xc" + end, j), "c", ("P", "X" + end, j))
    for name, link in (("zo", "z"), ("co", "c"), ("cz", "c")):
        t.add(("M", name, 0), link, {r: (r ^ 2 if name == "cz" else r, 0, 1) for r in EVERY})
    return t


TABLE = build_table()
NAMES = tuple(TABLE.rows)


def view(refs, array, area):
    row, col, wide = area
    if array == "M":
        return refs["M"].at[pl.ds(row * 8, 8), :]
    return refs[array].at[pl.ds(row * BLK, BLK), pl.ds(col * BLK, wide * BLK)]


class Role:
    def __init__(self, kind, role, refs, send_sem, recv_sem, cannon, panels):
        self.kind, self.role, self.refs = kind, role, refs
        self.send_sem, self.recv_sem = send_sem, recv_sem
        self.cannon, self.panels = cannon, panels

    def copy(self, row, sender):
        area = row.areas[sender]
        panel = self.cannon
        if row.link in "pP":
            panel = lax.rem(self.cannon + 1, self.panels)
        if row.link in "mM":
            panel = lax.rem(self.cannon + self.panels - 1, self.panels)
        return pltpu.make_async_remote_copy(
            src_ref=view(self.refs, row.array, area),
            dst_ref=view(self.refs, row.array, shift(area, row.link)),
            send_sem=self.send_sem.at[row.index],
            recv_sem=self.recv_sem.at[row.index],
            device_id=(panel, self.role ^ FLIP[row.link]),
            device_id_type=MESH,
        )

    def send_one(self, name):
        row = TABLE.rows.get(name)
        if row is not None and self.kind in row.senders and self.role in row.areas:
            self.copy(row, self.role).start()

    def recv_one(self, name):
        row = TABLE.rows.get(name)
        if row is None or self.kind not in row.receivers:
            return False
        sender = self.role ^ FLIP[row.link]
        if sender not in row.areas:
            return False
        self.copy(row, sender).wait_recv()
        return True

    def play(self, step):
        for entry in PLANS[self.kind, self.role][step]:
            name = NAMES[abs(entry) - 1]
            if entry > 0:
                self.recv_one(name)
            else:
                self.send_one(name)

    def drain(self):
        for row in TABLE.rows.values():
            if self.kind in row.senders and self.role in row.areas:
                self.copy(row, self.role).wait_send()


PLANS = {
    (0, 0): (
        (-309, -310, -1, -2, -5, -78, -79, -82, -170, -261, -263, -11, -88, -179, -266, -268, -47, -132, -223,
         -290, -293, 310, -173, 2, 79, 170, 261, 11, 88, 179, -169, 266, -14, 47, 309, -311, 132, 223, 290,
         -260, 263, -264, 1, -3, 5, -8, 268, -269, -10, 293, -294, 78, -80, 82, -85, -19, 311, -96, -6, 84,
         169, -171, 173, -176, 3, 8, -87, 175, 260, -262, 14, -17, -83, 264, -174, 93, 184, 80, -178, 85, -91,
         19, -20, 269, 171, -265, 176, -182, 96, -97, 10, -187, -12, 6, -9, 262, 17, -15, 87, -270, -89, 83,
         -86, 178, -180, 174, 9, -177, 20, -272, 138, -92, 97, 91, -94, 12, 94, -183, 188, 182, -185, 187,
         -188, 89, -58, 271, 15, -18, 270, -271,),
        (180, -68, -291,),
        (265, 267, 49, -267,),
        (21, 185, 229, 92, -71, -22, -95,),
        (183, -186, -147, 59, 294, -303, 58, -59, -60, -238, 22, 98, 51, -99, 68, -69, 18, 189, 99, -190, 272,
         -273, 148, 71, -72, 239, 48, -49, 147, -148, -149, 190, 238, -239, -240, 158, -50, 133, -134, 224,
         -225, 273,),
        (230, 303, -304, -135, -231,),
        (-226,),
        (162, 253, 55,),
        (140, 50, 231, -51, 295, -296, 249, 135, 296, -136, 226, -227,),
        (),
        (),
    ),
    (0, 1): (
        (-310, -2, -79, -170, -261, -11, -88, -179, -266, -47, -132, -223, -290, -309, -1, -5, -81, -172, -78,
         310, 2, -263, 79, 170, 261, 11, 88, 179, 266, 47, -90, 132, 223, 290, -181, -82, 311, -268, -173,
         309, -311, 81, 264, -84, 3, 8, -169, -14, 269, 1, -3, 5, -8, 172, 294, -175, 80, 85, -260, 263, -264,
         -19, -6, 90, -93, -137, 171, 176, -10, 181, -184, 78, -80, -96, 82, -85, 262, -87, 17, -91, 268,
         -269, 169, -171, -187, 173, -176, 260, -262, -270, 14, -17, 20, 6, -9, -178, 19, -20, 137, -138, 97,
         12, -265, 9, -182, -228, 96, -97, 89, -58, 10, -12, -293, 91, 86, -94, -98, 187, -188, 180, 177,
         -189, 87, -89, 270, -271, -272, 178, -180, -15, 94, -133, 265, -267, -224, 48, -49, -50, 185, -147,
         188, 182, -185, 228, -229, 18, -291, -238, 271,),
        (58, 293, -59, -60, -294,),
        (21, 50, 267, -157, -22, -51,),
        (15, 98, 22, -18, -99,),
        (95, 186, 147, -148, -149, -161, 59, 238, -239, -240, 99, -252, 69, 190, -248, 189, -190, 157, 273,
         -158, 72, 272, -273,),
        (49, 148,),
        (161, 252, 239, -162, -253,),
        (54, 134, -55,),
        (225, 139, -140, 304, 231, 230, -231, 248, -249, 295, -296, 51, 296, 136, 227,),
        (),
        (),
    ),
    (0, 2): (
        (-309, -310, -1, -2, -4, -5, -78, -79, -81, -82, -170, -261, -11, -88, -179, -266, -47, -132, -223,
         -290, -169, 310, -172, -173, 2, 79, 170, 261, 11, 88, 179, -260, 266, -14, 47, 309, -311, 132, 223,
         290, -263, -91, 1, -3, 4, 5, -7, -8, -13, -6, 78, -80, 81, 82, -84, -85, -83, 311, 173, -176, -10,
         172, -175, 8, 3, -87, 7, 17, -90, -182, 169, -171, 14, -17, 80, 59, -178, 260, -262, 263, 91, -264,
         -94, -270, -174, 84, 10, -12, 13, 6, -9, -16, -15, 83, -86, -58, -147, 171, 182, -185, 175, -181, 87,
         -89, 90, -93, 262, 9, -268, 264, 270, -271, -265, 174, -177, -21, 86, 97, -92, 12, 15, -18, 178,
         -180, -183, 89, 58, -59, 16, -228, 265, -267, -238, 147, 93, -148, 181, -184, -98, 188, -293, 268,
         -269, -189, 272, -273, 180, 177, -272, 267, 92, -95, 18, 99, 228, 183, 271, -186, -229,),
        (238, -48, -239,),
        (184, 190,),
        (273, 291, 293, -133, -292, -294,),
        (95, 269, 53, 134, -71, -303, -224, -230,),
        (186, 225, 60, -61,),
        (138, 292,),
        (158, 61, 229,),
        (162, -295, 150, 294, 303, -304, 249, 241, 149, -150, 253, 240, -241,),
        (71, -72,),
        (),
    ),
    (0, 3): (
        (-310, -2, -79, -170, -261, -11, -88, -179, -266, -47, -132, -223, -290, -309, -1, -4, -5, -14, 310,
         2, 79, 170, -58, 261, 11, 88, 179, -81, 266, 47, 132, 223, 290, -78, 311, -169, 309, -311, 3, 5, -8,
         -260, 7, -172, 8, 1, -3, 4, 14, -7, -17, 80, 84, -263, -6, 85, 78, -80, 58, -59, 81, 176, -84, -83,
         175, -96, 171, 17, -10, -13, 262, -87, 264, -90, 94, 169, -171, 172, -175, 12, -178, 9, -187, 16,
         260, -262, 263, 6, -9, -264, 86, -265, -174, 96, 83, -86, -97, -48, 10, -12, 185, -15, 89, 93, -270,
         87, -89, 13, -16, 271, -181, 90, -93, 177, -21, 187, -188, 18, -98, -268, 180, -92, 178, -180, 59,
         -52, 267, 174, -177, -183, 265, -267, 148, 15, 184, -18, -137, 98, -99, 270, -271,),
        (269, 189, 273, 181, -184, -189, -190, -228,),
        (272, -157, -161, -273, -293,),
        (95, 133, 268, 52, 92, 186, 229, -248, -252, -95, -269, -272, -53, -134,),
        (224, 183, 239, -186, -225,),
        (291, 137, -138, -292,),
        (60, 292, 228, 294, 157, -158, -54, -61, -139, -229,),
        (161, 293, 149, -162, -150, -230, -294,),
        (61, 248, 240, -249, -241, -295, 252, -253, 304, 150, 241,),
        (72,),
        (),
    ),
    (1, 0): (
        (-309, -310, -1, -2, -5, -78, -79, -82, -170, -261, -11, -88, -179, -266, -47, -132, -223, -290, 310,
         -173, 2, 79, 170, 261, 11, 88, 179, -169, 266, -14, 47, 309, -311, 132, 223, 290, -91, 263, -264, 1,
         -3, 268, -269, -6, 293, -294, 78, -80, -83, 311, -182, 84, 169, -171, 3, -174, 175, 260, -262, -260,
         264, 10, -12, 93, -10, 87, -89, 184, -87, 19, -20, 269, -178, 96, -97, 80, -265, 30, -31, 171, -272,
         -291, 20, -15, 138, 31, -92, 97, 262, -58, 188, 187, -188, 112, -147, 271, 111, -112, 203, -238, 33,
         -34, 229, 36, -41, 270, -271, 114, -115, -42, 294, 34, 51, 12,),
        (37, 202, 68, 205, -69, -71, -203, -206, -44, -45, 118, 89, -126, -127,),
        (41, 178, -180, -183, 119, -129, -130, 209, -217, -218, 265, -267, 210, -220, -221, 180,),
        (21, -22, 98, -99, 158, 44, 126, 303, -304, 217, 267,),
        (189, -190, 22, 272, -273, 50, -51, 48, -49, 249, 99, 135, -136, 64, -65, 226, -227, 133, -134, 74,
         -77, 153, -154, 224, -225, 230, -231, 190, 168, 244, -245, 273,),
        (295, 49, -296,),
        (),
        (),
        (259, 55, 65, 140, 231, 296,),
        (),
        (),
    ),
    (1, 1): (
        (-310, -2, -79, -170, -261, -11, -88, -179, -266, -47, -132, -223, -290, -309, -1, -5, -78, 310, 2,
         79, 170, 261, 11, 88, 179, 266, 47, 132, 223, 290, -169, 311, -260, 309, -311, 81, 264, -84, 3, -10,
         269, 1, -3, 172, 294, -175, 80, -87, 263, -264, -178, 90, -93, -6, 171, -82, 181, -184, 262, -173,
         268, -269, 12, -14, 78, -80, 89, -91, 169, -171, 20, -182, 19, -20, 137, -138, 97, -58, 30, -31, 96,
         -97, 31, -265, 260, -262, 187, -188, -98, 111, -112, -189, 270, -271, 202, -203, -272, -133, 228,
         -229, -224, 188, 293, -294, 33, -34, 112, -291, -147, 34, -238, 50, -51, 10, -12, 41, -15, 271,),
        (115, 36, 87, -89, -41, -42,),
        (-161, 69, 203, 206, 178, -180, 44, 126, 180,),
        (157, 129, 37, -158, -252, -44, -45, 217, 267, 118, 220, -126, -127, 209, -217, -218, 22, 265, -267,),
        (99, 21, -22, 304, 248, -249, 98, 190, -99, 273, 51, 49, 136, 65, 227, 134, 77, 154, 189, 225, -190,
         164, -168, 231, 272, -273,),
        (48, -49,),
        (),
        (255, 54, 245, -259, -55,),
        (64, -65, 139, 296, -140, 230, -231, 295, -296,),
        (),
        (),
    ),
    (1, 2): (
        (-309, -310, -1, -2, -5, -23, -78, -79, -82, -100, -170, -261, -11, -88, -179, -266, -47, -132, -223,
         -290, -169, 310, -173, -191, 2, 79, 170, 261, -14, 11, 88, 179, -260, 266, -274, 47, 309, -311, 132,
         223, 290, -10, -91, 1, -3, 4, -7, -87, -6, -35, 78, -80, 81, -84, 24, -29, -83, -116, 102, 311, -110,
         -182, -207, 172, -175, 3, 7, -30, 169, -171, -174, -282, 193, -201, 80, 29, 263, -264, -58, -56, 62,
         -66, 84, 13, -16, -147, -141, 171, -238, -232, 262, 110, -297, 175, -111, 12, 201, 90, -93, 25, -32,
         89, 264, -33, 260, 66, 181, -262, -184, 180, 270, -271, 103, 10, -113, -12, -114, 32, 268, -269, -15,
         87, -89, 228, -229, -275, 194, -204, 178, -180, 151, -155, 155, -92, 265, -267, 97, -202, 242, 272,
         -273, -246, -183, -283, 291, -292, -205, 188, -298, -178, 271,),
        (),
        (-265,),
        (267, 16, -70, -71, -21,),
        (93, 99, 246, 184, 190, -98, 293, -294, -305, 269, 273,),
        (53, 134, 67, 225, 42, -43, 292, 138, -189, 229, -272, 45, -46, 158, 43,),
        (127, 294, -128, -48, 63, 130, -131, -67, 303, 249, -304, -64, 218, -219, 221, -222, -133, -153, 73,
         -76, 46, -224, -230, 128,),
        (219,),
        (-244, 167, -295, 152, -156, 243, -247,),
        (258,),
        (),
    ),
    (1, 3): (
        (-310, -2, -79, -170, -261, -11, -88, -179, -266, -47, -132, -223, -290, -309, -1, -5, -23, -14, 310,
         2, 79, 170, 261, 11, 88, 179, 266, 47, 132, 223, -58, 290, -100, 311, 309, -311, 3, 7, -78, 1, -3, 4,
         -7, 80, 84, -169, 78, 29, -80, -6, 24, -29, -101, 81, 110, -84, 175, -30, 169, -171, 171, -260, 260,
         201, -262, 102, -110, 264, -111, 10, 66, 172, -175, -12, 193, -201, 16, -202, -83, 87, -89, 263,
         -264, 62, -66, -174, 178, -180, -191, -15, 25, -32, -192, 93, -33, -92, 32, -274, 262, 184, 151,
         -155, 271, -10, 96, 113, -97, 12, -183, -275, 269, -87, 89, 187, 229, -188, -35, 204, 180, 270, -271,),
        (155,),
        (267, 13, 265, 273, 246, 242, 98, 292, 90, -159, -161, -178, -267, -16, -93, -99, -246,),
        (189, 181, -184, -190,),
        (272, 268, -269, -273,),
        (133, 52, -53, -134, 63, 224, -67, -225, -265, 291, -292, 137, -138, -252, 294, -21, 228, -229, 157,
         -158, 42, -43, 43, 293, -294, -250, 248, -249, -98, 46,),
        (-116, 128, 131, 67, -117, 304, 45, -46, -207, 219, 127, 222, -128,),
        (-208, 218, -219,),
        (-189, -282, 76, -283, 163, -167, -272, -56, -48, -141, -142, -54, -232, -64, -139, 156, -233, 247,),
        (-230, -297, 254, -258, -295, -298,),
        (),
    ),
    (2, 0): (
        (-309, -310, -1, -2, -24, -78, -79, -102, -170, -261, -263, -11, -88, -179, -266, -268, -47, -132,
         -223, -290, -293, 310, -193, 2, 79, 170, 261, 11, 88, 179, -169, 266, -62, 47, 309, -311, 132, 223,
         290, -260, 1, -3, 5, -8, -10, 78, -80, 82, -85, 23, -19, -26, 311, 100, -96, -104, -27, -25, 173,
         -176, 3, 8, -105, 169, -171, 14, -17, -103, 191, -187, -195, 80, -196, 26, 274, -276, -194, 171, 85,
         -277, -151, 262, -87, 176, -242, 260, -262, 6, 104, -9, 12, -178, 17, -36, 10, -270, -12, 83, -86,
         87, -89, 174, 9, -177, -265, 107, -37, 56, -57, 91, -94, -291, 89, 94, -118, 141, -143, 182, -185,
         180, 232, -234, 15, -18, -119, 178, -180, 267, 49, 297, -299, -209, 265, -267, -210, 39, -40, 185,
         92, -95, 121, -122, 183, 195, -186, -301, 59, 212, 275, 198, -279, -213, 58, -59, 285, -286, 276, 18,
         48, -49, -50, -63, 279,),
        (133, 298, 148, 224, -68, -73, -280, -134, -225, -300,),
        (71, 239, -72,),
        (147, -148,),
        (238, -303, -239, 288, -289, 165, 70, -74, -75, 40, 162, -152, 253, -135, -243, -60, -149, 305, -307,
         -306, -240, -226, 256, 122, 125, 57, 213, 143, 216, 144, 286, 234, 289,),
        (),
        (235,),
        (299,),
        (300,),
        (),
        (),
    ),
    (2, 1): (
        (-310, -2, -79, -170, -261, -11, -88, -179, -266, -47, -132, -223, -290, -309, -1, -24, -81, -172,
         -78, 310, 2, -263, 79, 170, 261, 11, 88, 179, 266, 47, -90, 132, 223, 290, -181, -102, 311, -268,
         -193, 309, -311, 3, 8, -169, -62, 1, -3, 5, -8, 80, 85, 78, -80, 26, 23, -19, -26, -25, 104, 176,
         169, -171, 82, -85, -151, -96, 171, 17, -27, 260, -262, 173, 195, -176, 100, -104, -187, 10, -12, 14,
         276, -17, -270, -137, 6, -9, 262, -105, 9, -242, 101, -107, -228, 12, -36, 87, -89, -293, 91, 86,
         -94, 89, 177, -108, 178, -180, -260, 265, -267, 48, -49, -50, 57, -10, 94, -63, 143, -87, 185, 182,
         -185, 234, -178, 18, 191, -195, 180, 58, -59, 299, -196, -37, 192, -198, 267, -118, 274, -276, 40,
         15, -199, -18, -209, 95, 122, 186, -277, 275, -279, 147, 279, -280, -148,),
        (213, 59, 286, 238, -265, -239,),
        (49,),
        (-157, -60,),
        (134, -163, -133, 225, 300, 159, -165, -160, -149, 72, 39, -40, 161, 148, -162, -224, 252, -253, 239,
         -240, 289, -291, 75, -164, -248, -254, 307, -255, 250, -251, -256, 121, -122, 124, -125, 56, -57,
         212, -213, 141, -143, -145, 215, -216, 142, -144, 285, -286, 232, -234, -236, 288, -289,),
        (233, -235,),
        (297, -299, -301,),
        (298, -300,),
        (),
        (),
        (),
    ),
    (2, 2): (
        (-309, -310, -1, -2, -4, -78, -79, -81, -170, -261, -11, -88, -179, -266, -47, -132, -223, -290, 310,
         -172, 2, 79, 170, 261, 11, 88, 179, -169, 266, -263, 47, 309, -311, 132, 223, 290, -13, 1, -3, 5, -8,
         -90, 78, -80, 82, -85, 311, 173, -176, -260, 8, 3, 17, -10, 169, -171, 14, -17, -181, 80, 59, -87,
         260, -262, 91, -94, 10, -12, 6, -9, -270, 83, -86, -268, 27, -28, 35, -38, 171, 182, -185, -228, 105,
         -106, 116, -178, -120, -293, 9, 196, -197, 207, -265, -211, 174, -177, 86, -39, 15, -18, 282, -284,
         277, -278, -121, 28, 58, -59, 87, -89, -212, 147, -148, 178, -180, -285, -48, 265, -267, 177, -133,
         106, 291, -292, 18, -224, 92, -95, 109, 95, 183, -186, 262, 238, -239, 12, 186, 89, 283, -287, -288,
         301, -302, 180, 38, 197, 200, 278, 280, -281, 281,),
        (),
        (267,),
        (),
        (61, 134, -303, 166, 162, 150, 225, 60, -61, 241, 149, 253, -150, 292, 71, -72, 306, -308, 120, 240,
         -241, 123, 211, 214, 257, 284, 287,),
        (),
        (),
        (),
        (146, 237, 302,),
        (),
        (),
    ),
    (2, 3): (
        (-310, -2, -79, -170, -261, -11, -88, -179, -266, -47, -132, -223, -290, -309, -1, -4, -78, 310, 2,
         79, 170, 261, 11, 88, 179, 266, 47, 132, 223, 290, -169, 311, -260, 309, -311, 3, 5, -8, -10, 8, -81,
         1, -3, 14, -17, 80, 85, -172, 78, -80, 58, -59, -96, 176, -263, 171, 17, -87, 262, 94, -178, -13,
         169, -171, 12, 9, -265, 6, -9, 86, -48, 28, 83, -86, 38, 185, -187, 106, 120, 27, -28, -90, 197, 211,
         177, -181, 18, -268, 284, 278, 59, -52, 89, 174, -177, -137, 105, -106, 148, 180, 15, -18, -228, 108,
         -109, 92, -95, -293, 267, 260, -262, -270, 292, 10, -12, 95, 183, -186, 87, -89, 186, 178, -180, 35,
         -38, -39, 239, 196, -197, 287, 199, -200, 302, 277, -278, 280, -281, 265, -267, 60, -61, 133, 281,
         -134,),
        (160, -166,),
        (149, 161, -157, -162, -150,),
        (224, -248, -225,),
        (240, -241, 252, -253, 291, -292, 116, -120, -121, 117, -123, -124, 61, 150, 207, -211, -212, 208,
         -214, -215, 251, -257, 72, 308, 241, 282, -284, -285, 283, -287, -288,),
        (),
        (),
        (),
        (145, -146, 236, -237, 301, -302,),
        (),
        (),
    ),
}


def kernel(panels, root_in, inverse_in, hamilton_in, margin_in, hamilton_mask_in,
           root_out, inverse_out, lowdin_out,
           root, inverse, hamilton, poly, margin, next_rows, send_sem, recv_sem):
    cannon, rep = lax.axis_index("cannon"), lax.axis_index("rep")
    refs = {"R": root, "I": inverse, "H": hamilton, "P": poly, "M": margin}
    ahead, behind = lax.rem(cannon + 1, panels), lax.rem(cannon + panels - 1, panels)
    sibling, across = rep + 1 - 2 * lax.rem(rep, 2), lax.rem(rep + 2, 4)

    place = lax.rem(cannon, Z_PANELS)
    far = ((place == Z_PANELS - 1) & (rep >= 2)) | ((place == 0) & (rep < 2))
    beyond = lax.rem(cannon + jnp.where(place == 0, panels - 1, 1), panels)

    barrier = pltpu.get_barrier_semaphore()
    for peer in ((ahead, rep), (behind, rep), (cannon, sibling), (cannon, across)):
        pl.semaphore_signal(barrier, inc=1, device_id=peer, device_id_type=MESH)

    @pl.when(far)
    def _():
        pl.semaphore_signal(barrier, inc=1, device_id=(beyond, across), device_id_type=MESH)

    for array, source, scale in (
        (root, root_in, margin_in), (inverse, inverse_in, margin_in), (hamilton, hamilton_in, hamilton_mask_in),
    ):
        for j in range(ROWS):
            for b in range(2):
                keep = scale[b, j].astype(jnp.float32).astype(jnp.bfloat16)
                at = pl.multiple_of((j + 2 * rep + b) * BLK, BLK)
                array[pl.ds((j + HALF) * BLK, BLK), pl.ds(at, BLK)] = source[j, b] * keep
    for j in range(ROWS):
        for b in range(2):
            keep = margin_in[b, j].astype(jnp.float32)
            margin[pl.ds(rep * 8 + j * 2 + b, 1), :] = jnp.full((1, BLK), keep, jnp.float32)
    for array in (root, inverse, hamilton, poly):
        for row in range(SPAN):
            right = row + HALF
            if right < SPAN:
                array[row * BLK:(row + 1) * BLK, right * BLK:] = jnp.zeros((BLK, (SPAN - right) * BLK), jnp.bfloat16)
            left = row - HALF
            if left > 0:
                array[row * BLK:(row + 1) * BLK, :left * BLK] = jnp.zeros((BLK, left * BLK), jnp.bfloat16)

    @pl.when(far)
    def _():
        pl.semaphore_wait(barrier, 5)

    @pl.when(jnp.logical_not(far))
    def _():
        pl.semaphore_wait(barrier, 4)

    def by_role(plan):
        for kind in KINDS:
            here = {PLAIN: (place > 0) & (place < Z_PANELS - 1), LAST: place == Z_PANELS - 1, FIRST: place == 0}[kind]
            for role in EVERY:
                @pl.when(here & (rep == role))
                def _():
                    plan(Role(kind, role, refs, send_sem, recv_sem, cannon, panels))


    def mask_row(i):
        return jnp.concatenate([margin[(t // 2) * 8 + i * 2 + t % 2:(t // 2) * 8 + i * 2 + t % 2 + 1, :]
                                for t in range(NS)], axis=1)

    def window(i):
        return slice(i * BLK, (i + NS) * BLK)

    def own(i):
        return slice((i + HALF) * BLK, (i + HALF + 1) * BLK)

    at_row = lax.broadcasted_iota(jnp.int32, (BLK, NS * BLK), 0)
    at_col = lax.broadcasted_iota(jnp.int32, (BLK, NS * BLK), 1)
    for i in range(ROWS):
        by_role(lambda d: d.play(i))
        product = jnp.dot(inverse[own(i), window(i)], root[window(i), window(i)], preferred_element_type=jnp.float32)
        diagonal = jnp.where(at_col - HALF * BLK == at_row, 1.5, 0.0).astype(jnp.float32)
        poly[own(i), window(i)] = (diagonal - 0.5 * (product * mask_row(i))).astype(jnp.bfloat16)

    for i in range(ROWS):
        by_role(lambda d: d.play(ROWS + i))
        product = jnp.dot(poly[own(i), window(i)], inverse[window(i), window(i)], preferred_element_type=jnp.float32)
        next_rows[i] = (product * mask_row(i)).astype(jnp.bfloat16)
        mine = next_rows[i, :, pl.ds(pl.multiple_of(2 * rep * BLK, 2 * BLK), 2 * BLK)]
        for b in range(2):
            inverse_out[i, b] = mine[:, b * BLK:(b + 1) * BLK]

    def narrow(first, second, i):
        cols = pl.ds(pl.multiple_of((i + 2 * rep) * BLK, BLK), 2 * BLK)
        return jnp.dot(first, second[window(i), cols], preferred_element_type=jnp.float32)

    by_role(lambda d: d.play(2 * ROWS))
    for i in range(ROWS):
        product = narrow(next_rows[i], hamilton, i)
        for b in range(2):
            keep = hamilton_mask_in[b, i].astype(jnp.float32)
            lowdin_out[i, b] = (product[:, b * BLK:(b + 1) * BLK] * keep).astype(jnp.bfloat16)

    by_role(lambda d: d.play(2 * ROWS + 1))
    for i in range(ROWS):
        product = narrow(root[own(i), window(i)], poly, i)
        for b in range(2):
            keep = margin_in[b, i].astype(jnp.float32)
            root_out[i, b] = (product[:, b * BLK:(b + 1) * BLK] * keep).astype(jnp.bfloat16)

    def finish(d):
        d.play(2 * ROWS + 2)
        d.drain()

    by_role(finish)


def solution(mesh):
    panels = mesh.shape["cannon"]
    count = len(TABLE.rows)
    vmem = pl.BlockSpec(memory_space=pltpu.VMEM)
    smem = pl.BlockSpec(memory_space=pltpu.SMEM)

    def body(root_margin, inverse_root, hamiltonian, margin_mask, hamilton_mask):
        shape = jax.ShapeDtypeStruct(root_margin.shape, jnp.bfloat16)

        def run(*refs):
            kernel(panels, *refs)

        band = pltpu.VMEM((SPAN * BLK, SPAN * BLK), jnp.bfloat16)
        return pl.pallas_call(
            run,
            out_shape=(shape, shape, shape),
            in_specs=[vmem, vmem, vmem, smem, smem],
            out_specs=(vmem, vmem, vmem),
            scratch_shapes=[
                band, band, band, band,
                pltpu.VMEM((4 * 8, BLK), jnp.float32),
                pltpu.VMEM((ROWS, BLK, NS * BLK), jnp.bfloat16),
                pltpu.SemaphoreType.DMA((count,)),
                pltpu.SemaphoreType.DMA((count,)),
            ],
            compiler_params=pltpu.CompilerParams(
                collective_id=0, has_side_effects=True, vmem_limit_bytes=48 << 20
            ),
            cost_estimate=pl.CostEstimate(flops=4 * 4 * 268435456, bytes_accessed=6 * 262144, transcendentals=0),
            name="newton_step",
        )(root_margin, inverse_root, hamiltonian, margin_mask.T, hamilton_mask.T)

    spec = P("cannon", "rep", None, None)
    mask = P("cannon", "rep")
    return jax.shard_map(body, mesh=mesh, in_specs=(spec, spec, spec, mask, mask),
                         out_specs=(spec, spec, spec), check_vma=False)
```

```python
import jax
import jax.numpy as jnp
from jax import lax
from jax.experimental import pallas as pl
from jax.experimental.pallas import tpu as pltpu
from jax.sharding import PartitionSpec as P

MESH = pl.DeviceIdType.MESH
BLK = 128
NS = 8
HALF = 4
ROWS = 4
Z_PANELS = 32
SPAN = ROWS + NS - 1


def rect(j, slots):
    return (j + HALF, j + min(slots), len(slots)) if slots else None


def slots_of(role):
    return (2 * role, 2 * role + 1)


def pick(role, allowed):
    return [u for u in slots_of(role) if u in allowed]


def need_up(j):
    return range(HALF - j, NS)


def need_down(j):
    return range(0, NS - 1 - j) if j < 3 else ()


def shift(area, link):
    move = {"p": -ROWS, "P": -ROWS, "m": ROWS, "M": ROWS}.get(link, 0)
    return (area[0] + move, area[1] + move, area[2])


EVERY = (0, 1, 2, 3)
FLIP = {"c": 1, "z": 2, "p": 0, "m": 0, "P": 2, "M": 2}
PLAIN, LAST, FIRST = 0, 1, 2
KINDS = (PLAIN, LAST, FIRST)
ENDS = {
    (None, False): (KINDS, KINDS),
    ("p", False): ((PLAIN, FIRST), (PLAIN, LAST)),
    ("p", True): ((LAST,), (FIRST,)),
    ("m", False): ((PLAIN, LAST), (PLAIN, FIRST)),
    ("m", True): ((FIRST,), (LAST,)),
}


class Message:
    def __init__(self, array, link, areas, index, senders, receivers):
        self.array, self.link, self.areas, self.index = array, link, areas, index
        self.senders, self.receivers = senders, receivers


class Table:
    def __init__(self):
        self.rows = {}

    def put(self, name, array, link, areas, senders, receivers):
        areas = {role: area for role, area in areas.items() if area is not None}
        if areas:
            self.rows[name] = Message(array, link, areas, len(self.rows), senders, receivers)

    def add(self, name, link, areas, far=False):
        way = link.lower() if link in "pPmM" else None
        self.put(name, name[0], link, areas, *ENDS[way, far])

    def relay(self, name, link, of, roles=EVERY, keep=None):
        row = self.rows.get(of)
        if row is None:
            return
        got = {}
        for role in roles:
            sender = role ^ FLIP[row.link]
            if sender in row.areas:
                area = shift(row.areas[sender], row.link)
                got[role] = area if keep is None else keep(area)
        senders = row.receivers
        receivers = senders
        if link in "pm":
            ends = ENDS[link, False]
            senders, receivers = tuple(k for k in ends[0] if k in senders), ends[1]
        self.put(name, name[0], link, got, senders, receivers)


def within(area, low, high):
    first, end = max(area[1], low), min(area[1] + area[2], high)
    return (area[0], first, end - first) if end > first else None


def build_table():
    t = Table()
    for j in range(ROWS):
        low, high = range(HALF - j, HALF), range(HALF, NS - 1 - j)
        up, down = need_up(j), need_down(j)
        own = {r: rect(j, slots_of(r)) for r in EVERY}

        def some(allowed, roles=EVERY, other=0):
            return {r: rect(j, pick(r ^ other, allowed)) for r in roles}

        for a in "RI":
            t.add((a, "zo", j), "z", own)
            t.add((a, "co", j), "c", own)
            t.relay((a, "cz", j), "c", (a, "zo", j))
            t.add((a, "po", j), "p", some(up))
            t.add((a, "mo", j), "m", some(down))
            t.add((a, "mz", j), "m", some(down, EVERY, 2))
            t.relay((a, "cpo", j), "c", (a, "po", j))
            t.relay((a, "cmo", j), "c", (a, "mo", j))
            t.relay((a, "cmz", j), "c", (a, "mz", j))
        t.add(("R", "pz", j), "p", some(up, EVERY, 2))
        t.relay(("R", "cpz", j), "c", ("R", "pz", j))
        t.relay(("I", "zpo", j), "z", ("I", "po", j))
        t.relay(("I", "czpo", j), "c", ("I", "zpo", j))
        for a, plus, minus in (("R", "P", "M"), ("I", "p", "m")):
            t.add((a, "Xpo", j), plus, some(up, (2, 3)), True)
            t.add((a, "Xpz", j), plus, some(up, (2, 3), 2), True)
            t.add((a, "Xmo", j), minus, some(down, (0, 1)), True)
            t.add((a, "Xmz", j), minus, some(down, (0, 1), 2), True)
            for end in ("po", "pz", "mo", "mz"):
                t.relay((a, "Xc" + end, j), "c", (a, "X" + end, j))
                t.relay((a, "Xz" + end, j), "z", (a, "X" + end, j))
                t.relay((a, "Xcz" + end, j), "c", (a, "Xz" + end, j))

        t.add(("H", "co", j), "c", own)
        t.add(("H", "zo", j), "z", {r: rect(j, pick(r, low if r < 2 else high)) for r in EVERY})
        t.relay(("H", "cz", j), "c", ("H", "zo", j))
        t.relay(("H", "pz", j), "p", ("H", "zo", j), (0, 1))
        t.relay(("H", "cpz", j), "c", ("H", "pz", j))
        beyond = range(NS - 1 - j, NS)
        t.add(("H", "po", j), "p", {r: rect(j, pick(r, low if r < 2 else beyond)) for r in EVERY})
        t.relay(("H", "cpo", j), "c", ("H", "po", j))
        t.relay(("H", "zpo", j), "z", ("H", "po", j), (2, 3))
        t.relay(("H", "czpo", j), "c", ("H", "zpo", j))
        t.add(("H", "Xpo", j), "P", some(up, (2, 3)), True)
        t.add(("H", "Xpz", j), "P", some(low, (2, 3), 2), True)
        t.relay(("H", "Xcpo", j), "c", ("H", "Xpo", j))
        t.relay(("H", "Xcpz", j), "c", ("H", "Xpz", j))
        t.relay(("H", "Xzpo", j), "z", ("H", "Xpo", j), EVERY, lambda area: within(area, HALF, SPAN))
        t.relay(("H", "Xczpo", j), "c", ("H", "Xzpo", j))
        if j < 3:
            t.add(("H", "mo", j), "m", {r: rect(j, pick(r, range(HALF) if r < 2 else high)) for r in EVERY})
            t.relay(("H", "cmo", j), "c", ("H", "mo", j))
            t.relay(("H", "zmo", j), "z", ("H", "mo", j), (0, 1), lambda area: within(area, area[0] - HALF + 1, SPAN))
            t.relay(("H", "czmo", j), "c", ("H", "zmo", j))
            t.add(("H", "Xmo", j), "M", some(range(HALF), (0, 1)), True)
            t.add(("H", "Xmz", j), "M", some(high, (0, 1), 2), True)
            t.relay(("H", "Xzmo", j), "z", ("H", "Xmo", j), EVERY, lambda area: within(area, 0, area[0] - HALF + 3 - j))
            t.relay(("H", "Xczmo", j), "c", ("H", "Xzmo", j))
            for end in ("mo", "mz"):
                t.relay(("H", "Xc" + end, j), "c", ("H", "X" + end, j))

        core = 0 if j in (0, 3) else 1
        wide, few = rect(j, up), rect(j, range(NS - j, NS))
        t.add(("P", "p", j), "p", {core: wide, 2 + core: few})
        t.relay(("P", "cp", j), "c", ("P", "p", j))
        t.add(("P", "Xp", j), "P", {2 + core: wide}, True)
        t.relay(("P", "Xq", j), "z", ("P", "Xp", j), EVERY, lambda area: within(area, HALF, SPAN))
        if j < 3:
            few, wide = rect(j, range(0, 3 - j)), rect(j, range(1, NS - 1 - j))
            t.add(("P", "m", j), "m", {core: few, 2 + core: wide})
            t.relay(("P", "cm", j), "c", ("P", "m", j))
            t.add(("P", "Xm", j), "M", {core: wide}, True)
            t.add(("P", "Xn", j), "m", {core: few}, True)
        for end in ("p", "q", "m", "n"):
            t.relay(("P", "Xc" + end, j), "c", ("P", "X" + end, j))
    for name, link in (("zo", "z"), ("co", "c"), ("cz", "c")):
        t.add(("M", name, 0), link, {r: (r ^ 2 if name == "cz" else r, 0, 1) for r in EVERY})
    return t


TABLE = build_table()
NAMES = tuple(TABLE.rows)


def view(refs, array, area):
    row, col, wide = area
    if array == "M":
        return refs["M"].at[pl.ds(row * 8, 8), :]
    return refs[array].at[pl.ds(row * BLK, BLK), pl.ds(col * BLK, wide * BLK)]


class Role:
    def __init__(self, kind, role, refs, send_sem, recv_sem, cannon, panels):
        self.kind, self.role, self.refs = kind, role, refs
        self.send_sem, self.recv_sem = send_sem, recv_sem
        self.cannon, self.panels = cannon, panels

    def copy(self, row, sender):
        area = row.areas[sender]
        panel = self.cannon
        if row.link in "pP":
            panel = lax.rem(self.cannon + 1, self.panels)
        if row.link in "mM":
            panel = lax.rem(self.cannon + self.panels - 1, self.panels)
        return pltpu.make_async_remote_copy(
            src_ref=view(self.refs, row.array, area),
            dst_ref=view(self.refs, row.array, shift(area, row.link)),
            send_sem=self.send_sem.at[row.index],
            recv_sem=self.recv_sem.at[row.index],
            device_id=(panel, self.role ^ FLIP[row.link]),
            device_id_type=MESH,
        )

    def send_one(self, name):
        row = TABLE.rows.get(name)
        if row is not None and self.kind in row.senders and self.role in row.areas:
            self.copy(row, self.role).start()

    def recv_one(self, name):
        row = TABLE.rows.get(name)
        if row is None or self.kind not in row.receivers:
            return False
        sender = self.role ^ FLIP[row.link]
        if sender not in row.areas:
            return False
        self.copy(row, sender).wait_recv()
        return True

    def play(self, step):
        for entry in PLANS[self.kind, self.role][step]:
            name = NAMES[abs(entry) - 1]
            if entry > 0:
                self.recv_one(name)
            else:
                self.send_one(name)

    def drain(self):
        for row in TABLE.rows.values():
            if self.kind in row.senders and self.role in row.areas:
                self.copy(row, self.role).wait_send()


PLANS = {
    (0, 0): (
        (-309, -310, -1, -2, -5, -78, -79, -82, -169, -170, -173, -260, -261, -263, -10, -11, -88, -179, -266,
         -14, -91, -268, -47, -132, -223, -290, -293, 310, 2, 79, 170, -87, 261, -182, 11, 88, 179, 266, 47,
         132, 309, -311, 223, -178, -58, 290, 263, 1, -3, -264, -265, 5, -8, 268, -269, 293, 78, -80, -272,
         -294, 82, -85, -19, -291, 169, -171, 173, -6, -176, -96, 84, 260, -262, 14, -83, -17, -187, 10, 175,
         91, -12, -94, -270, 264, -174, 311, 93, -15, 182, -185, 3, -147, 184, 8, 87, -89, 58, -59, 80, -92,
         269, 138, 178, -180, -60, 265, 229, -267, -183, 19, -20, 85, 48, 294, 6, -9, -49, -50, 96, -97, 176,
         133, -134, -135, 83, -86, 187, 224, -188, -225, -226, -238, 270, -271, 174, -177, 21, -22, 15, -18,
         17, 171, 147, -148, -149, 20, 50, 98, -99, -51, 92, -95, 97, 262, 135, -136, 183, -186, 226, -227,
         189, -190, 9, 12, 94, 272, 188, 238, -273, -239, -240, 230, -231, 89, 185, 271,),
        (-68, -71,),
        (180,),
        (59, 148, 295, -296, 267,),
        (18, 22, 239, -303, 99, 71, -72, 162, 190, 273,),
        (68, -69,),
        (158, 253, 49, 55,),
        (140,),
        (231, 296, 249, 303, -304, 51,),
        (),
        (),
    ),
    (0, 1): (
        (-310, -2, -79, -81, -170, -172, -261, -263, -11, -88, -179, -266, -90, -47, -132, -223, -290, -181,
         -309, -1, -5, 310, 2, 79, -268, 170, 261, 11, 88, 179, 266, 47, 132, -137, 223, 290, -228, -82, 311,
         -293, -173, 81, -84, 3, 264, 8, 269, -78, 172, -175, 80, 294, 85, -169, 263, -264, 171, 176, 90, 309,
         -311, -260, -14, -93, 262, 17, 181, 1, -3, -10, -184, 5, -8, -19, 12, 94, 268, 78, -80, -87, -269,
         137, -138, -96, -178, 228, -229, 185, 82, -85, 293, -294, -265, 89, -6, 59, 173, -176, -98, 180, -91,
         -189, 267, -182, 20, -272, 9, 49, 97, 14, -17, -133, 169, -171, -187, -58, -224, 134, 86, 188, 225,
         19, -20, -291, -147, 271, 177, 96, 260, -97, -262, -270, -238, 22, 18, 6, -9, 148, 10, -12, -15, 99,
         51, 95, 91, -94, 187, -188, 136, 186, 227, 87, -89, 182, -185, 270, -271,),
        (190,),
        (58, 178, 273, 239, 231, 147, -157, -161, -180, -59, -60, -148, -149,),
        (265, 238, 21, 15, -248, -252, -267, -18, -22, -239, -240,),
        (98, -99, 161, -162, 189, -190, 296, 272, -273,),
        (157, 48, 252, 54, -158, -253, -49, -55,),
        (72, 139, -50, -140,),
        (230, 295, -231, -296,),
        (69, 248, -249, 50, -51,),
        (304,),
        (),
    ),
    (0, 2): (
        (-309, -310, -1, -2, -4, -5, -78, -79, -81, -82, -169, -170, -172, -173, -260, -261, -263, -10, -11,
         -88, -179, -266, -13, -14, -91, -182, -47, -58, -132, -223, -290, 310, 2, 79, 170, 261, -90, -147,
         11, 88, 179, 266, 47, 132, 309, -311, 223, -87, -181, -238, 290, 1, -3, -178, -268, 4, 5, -6, -7, -8,
         78, -80, -265, -228, 81, 82, -83, -84, -85, 173, -176, -293, 169, -171, -48, 172, -174, -175, 14,
         -17, 260, -262, -133, 263, -264, 91, -270, -94, 10, -12, -224, 13, 182, -15, -16, -185, 58, -59, 311,
         -21, 87, -89, 90, 147, -92, -93, -148, 3, 238, -239, 7, 178, -180, 181, -184, -183, -98, 265, -267,
         268, 6, -9, -269, 272, -273, 228, 8, -229, 291, -292, 83, -86, -189, 293, -294, 174, -177, 270, -271,
         -272, 80, 15, -18, 84, 17, -230, 171, 59, 262, 175, 92, -95, 12, 9, 264, 183, -186, 60, -61, 89, 16,
         -295, 180, 93, 86, 184, 267, 177, 99, 269, 97, 190, 18, 53, 273, 188, 95, 134, 271,),
        (186, 149, 240, -71, -150, -241,),
        (138, 225, 292,),
        (229, 294,),
        (-303,),
        (61,),
        (158, 71, 150, -72,),
        (249, 241,),
        (303, -304,),
        (162, 253,),
        (),
    ),
    (0, 3): (
        (-310, -2, -79, -170, -261, -11, -88, -179, -266, -47, -132, -223, -290, -309, -1, -4, 310, 2, 79,
         -78, 170, 261, 11, 88, 179, 266, 47, 132, 223, 290, -5, 311, 3, 7, 8, 80, -81, 84, 85, 176, -14, 171,
         -58, 175, 309, -311, -172, 17, -169, 262, 264, 1, -3, 4, -7, -263, -6, 94, 12, 16, 185, -13, -260,
         59, 5, -8, -90, 89, 93, 148, 239, -181, -10, 180, 184, -268, 267, 9, 269, 78, 273, -80, -83, -96,
         229, 292, -87, 81, 14, 86, -84, -17, -52, 169, -171, -174, 58, 294, -187, -59, 177, 260, -262, 172,
         -175, -270, 271, 10, -12, -178, -15, -137, 263, 6, -9, -264, 18, 87, -89, -265, -92, -228, 13, -16,
         178, -180, -21, -183, -293, 90, -93, 95, 181, 83, -86, -184, 265, -267, 186, 98, 61, 268, 174, -177,
         -98, -99, -269, 96, -97, 189, -189, -190, 52, 15, -18, -53, 272, -272, -273, 187, 92, -188, -95, 133,
         -134, -48, 270, 183, -271, -186,),
        (224, 137, 291, -54, -138, -139, -225, -292,),
        (228, 293, -157, -161, -229, -230, -294, -295,),
        (-248, -252,),
        (150, 241, 60, -61,),
        (157, 149, -158, -150,),
        (240, 248, -249, -241,),
        (),
        (),
        (161, 72, -162, 252, -253, 304,),
        (),
    ),
    (1, 0): (
        (-309, -310, -1, -2, -5, -78, -79, -82, -169, -170, -173, -260, -261, -10, -11, -88, -179, -266, -14,
         -91, -47, -132, -223, -290, 310, 2, 79, 170, 261, 11, 88, 179, 266, 47, 132, 309, -311, 223, -87,
         -182, 290, 263, 1, -3, -264, -178, 268, -269, 293, 78, -80, -265, -294, 169, -171, -272, -291, 84,
         260, -262, -6, 10, 175, -12, 264, -83, 311, 93, -174, 3, -15, 184, 87, -89, 80, -92, 269, 138, 178,
         -180, 36, -41, -183, 265, 229, -267, -42, -58, 118, -126, 19, -20, 294, -147, 96, -97, 187, -188,
         -127, 171, -238, 270, -271, 262, 209, -217, 12, 89, 37, -44, 20, 50, -51, 180, 97, -45, 135, 30, -31,
         -136, 267, 226, 49, -218, -227, 119, -129, 33, -34, -130, 111, -112, 210, -220, -221, 114, 188, -115,
         202, 271, -203,),
        (205, -71, -206, 31,),
        (21, -22, 34, 112,),
        (41, 44, 126, 203,),
        (98, -99, 22, 189, -190, 217, 158, 68, -69, 272, -273, 99, 48, -49, 64, -65, 74, -77, 249, 190, 133,
         -134, 303, -304, 273,),
        (153, -154,),
        (224, 230, 51, 55, -225, -231,),
        (244, -245,),
        (168, 65, 295, -296, 259, 140, 231, 296,),
        (),
        (),
    ),
    (1, 1): (
        (-310, -2, -79, -170, -261, -11, -88, -179, -266, -47, -132, -223, -290, -309, -1, -5, 310, 2, 79,
         170, -78, -82, 261, 11, 88, 179, 266, 47, 132, 223, 290, -173, 311, -14, 81, -84, 3, 264, 269, -91,
         172, -175, 80, 294, -169, 263, -264, 171, 90, 309, -311, -260, -93, -182, 262, 181, 1, -3, -10, -184,
         12, 268, 78, -80, -87, -269, 137, -138, -178, 228, -229, -265, 293, -294, 89, 180, 41, 169, -171,
         -98, -189, 267, 126, 260, 20, -262, -6, 10, 97, -12, -272, -15, 87, 188, -89, -58, 19, -20, -133,
         178, 271, -180, -147, -224, 217, 96, -97, 265, -267, -291, -238, 48, -49, 44, 51, 187, -188, 31, 136,
         227, 129, 270, -271,),
        (34, 112, 220, 115, 30, -31,),
        (203, 33, 206, -161, -34, 111, -112,),
        (36, 37, -252, -41, -42, -44, -45, 118, -126, -127, 202, -203,),
        (209, 22, 21, -22, -217, -218, 157, -158, 98, -99, 99, 190, 69, 273, 248, -249, 189, -190, 49, 272,
         -273,),
        (65, 77,),
        (54, 50, 134, -51, -55,),
        (164, 64, 304, -168, -65,),
        (154, 255, 139, -259, -140, 225, 231, 245, 230, -231, 295, 296, -296,),
        (),
        (),
    ),
    (1, 2): (
        (-309, -310, -1, -2, -5, -23, -78, -79, -82, -100, -169, -170, -173, -191, -260, -261, -274, -10, -11,
         -88, -179, -266, -14, -35, -91, -182, -47, -58, -132, -223, -290, 310, 2, 79, 170, 261, -147, 11, 88,
         179, 266, 47, 132, 309, -311, 223, -87, -238, 290, -116, 1, -3, -178, 4, -6, -7, -207, 78, -80, -265,
         81, -83, -84, -282, 24, -29, 169, -171, 172, -174, -175, -56, 102, -110, 260, -262, 263, -264, -275,
         193, -201, 10, -12, 13, -15, -16, 62, -66, 151, -155, 311, -141, 90, -93, 242, -246, 3, -232, 7, 87,
         -89, 181, -92, -184, 80, -297, 178, -180, 268, -183, -269, -30, 228, -229, 265, -267, 25, 272, -32,
         -33, -273, 293, -294, 291, -292, 103, -113, -111, 194, -204, -114, 84, -202, 171, 175, -205, 262,
         270, -271, 264, 29, -283, 12, 16, 89, 32, -21, 180, 93, 42, 110, -43, 267, 184, 269, 97, 201, 99,
         127, -98, -128, 53, 190, 66, -189, 188, 63, -67, -298, 155, 271,),
        (-70, -71, -272,),
        (273, 134, 138, 45, -46, -48,),
        (225, 218, 229, 246, 292, 294, 130, -131, -219, -64,),
        (152, 221, 243, -222, -133, -156, -247,),
        (158, -153, 67, -305, 249, 43,),
        (303, -304, -224, -230, -244, 73, 46, 128, -76,),
        (-295, 219,),
        (),
        (167, 258,),
        (),
    ),
    (1, 3): (
        (-310, -2, -79, -170, -261, -11, -88, -179, -266, -47, -132, -223, -290, -309, -1, -23, 310, 2, 79,
         -78, 170, -100, 261, 11, 88, 179, 266, 47, 132, 223, 290, -5, 311, 3, 7, -169, 80, 84, 29, -260, -14,
         171, -58, -191, 175, 309, 110, -311, -10, 262, -274, 264, 1, 201, 4, -3, -6, -7, -87, 12, 16, 78, 66,
         -80, -83, -178, 155, -265, 93, 246, -48, 89, -101, 184, -35, 180, 269, 229, -116, 267, 81, -84, 169,
         -171, -174, 32, 273, -192, 294, 292, 172, -175, 260, 113, -262, -275, 204, 263, -264, 24, 10, -29,
         -12, -15, -207, 13, -16, 87, -30, -89, -92, -117, 25, -32, 178, -33, -180, -183, -208, 90, -93, 102,
         -110, -111, 271, 265, -267, 181, -184, -282, 268, -269, -283, 193, 98, 96, -97, -201, -202, -99, 52,
         -53, -56, 189, -21, -190, 43, 62, -66, 187, -188, -141, 151, -155, 270, -271, -232,),
        (272, 133, 137, 128, -98, -273, -134, -138, -142,),
        (242, 224, 228, 67, 291, 293, -161, -225, -229, -246, -292, -294,),
        (-159, -252, -189,),
        (46,),
        (157, -158, -250, -272, 131, 219, 63, -67, 248, -249, -54, 42, -43,),
        (222, 156, 247, 45, 127, -46, -128, -64,),
        (218, -219,),
        (-139,),
        (304, 76, -230, -233, -297, -295, -298, 163, -167, 254, -258,),
        (),
    ),
    (2, 0): (
        (-309, -310, -1, -2, -24, -78, -79, -102, -169, -170, -193, -260, -261, -263, -10, -11, -88, -179,
         -266, -268, -47, -62, -132, -151, -223, -242, -290, -293, 310, 2, 79, 170, -87, 261, -36, 11, 88,
         179, 266, 47, 132, 309, -311, 223, -178, -118, 290, 1, -3, -265, 5, -8, -25, 78, -80, -291, 82, -85,
         -103, 23, -19, -26, -27, 169, -171, 173, -176, -194, 100, -96, -104, -105, -209, 260, -262, 14, -17,
         191, -187, -195, -196, 10, -12, 91, -94, 274, -270, -276, -277, -37, 311, 182, -185, 3, 8, 87, -89,
         58, -59, -119, 80, 178, -180, 26, -60, 265, -267, 104, -210, 85, 48, -49, -50, 6, -9, 176, 133, -134,
         -135, 83, -86, 224, 56, -57, -63, -225, -226, 275, -279, -280, 174, -177, 15, -18, 17, 171, 147, 195,
         -148, 141, -143, 262, 39, -40, -149, 92, 276, -95, 232, -234, 12, 183, -186, 297, -299, -301, -152,
         121, -122, 9, 89, -243, 212, -213, 107, 94, 285, -286, 238, -239, 185, 198, 180, 59, -240, 279,),
        (267, 148, -68, -73, -74,),
        (18, 40, 49, 239,),
        (122, 71, -72,),
        (162, 288, -303, -289, 253, 125, 213, 57, 298, -300, 143, 216, 234, 286, 144, 70, -75, 289,),
        (),
        (),
        (),
        (165, 256, 305, -306, -307, 235, 299, 300,),
        (),
        (),
    ),
    (2, 1): (
        (-310, -2, -79, -81, -170, -172, -261, -263, -11, -88, -179, -266, -90, -47, -132, -223, -290, -181,
         -309, -1, 310, 2, 79, -268, 170, 261, 11, 88, 179, 266, 47, 132, -137, 223, 290, -228, 311, -293, 3,
         8, 80, 85, 26, 171, -24, 176, 309, -311, 104, 262, 17, 1, -3, 5, 195, -8, -19, -78, 12, -25, 94, 78,
         -80, 276, -102, 23, -26, -27, -96, 100, -104, -105, 185, 82, -85, -193, 89, 59, -169, 173, -176, 180,
         -62, -260, 267, -151, -10, 49, 9, 14, -17, 169, -171, -187, -87, -242, 134, 86, 191, -195, 57, 225,
         260, 279, -196, -262, -270, -36, 274, -276, 177, 10, -277, -12, -37, -118, 18, -178, 6, -9, -209,
         148, 87, -89, 143, 40, 95, 101, -107, -108, 91, 234, -94, -265, 186, 182, 299, -185, -133, 122, -224,
         213, 178, 192, 58, -198, -199, -180, -59, 286, 239, 265, 275, 147, -279, -280, -267, -148,),
        (48, 238, 15, 39, -18, -40, -49, -50, -60, -63, -239,),
        (121, -157, -122, -149,),
        (161, -162, -163, -248, -240, -291,),
        (212, 56, 124, 252, -164, -253, -125, -213, -57, -254, 141, -143, -145, 72, 215, -216, 232, -234,
         -236, 285, -286, 289, -255, 142, -144, 288, -289,),
        (300,),
        (),
        (75,),
        (159, -160, -165, 250, -251, -256, 233, -235, 307, 297, -299, -301, 298, -300,),
        (),
        (),
    ),
    (2, 2): (
        (-309, -310, -1, -2, -4, -78, -79, -81, -169, -170, -172, -260, -261, -263, -10, -11, -88, -179, -266,
         -13, -47, -132, -223, -290, 310, 2, 79, 170, 261, 11, 88, 179, 266, 47, 132, 309, -311, 223, -87,
         -90, 290, 1, -3, -178, -181, 5, -8, 78, -80, -265, -268, 82, -85, 173, -176, 169, -171, -48, 14, -17,
         260, -262, -133, 91, -94, 10, -12, -224, 182, -270, -185, 58, -59, 311, 87, -89, 147, -148, 35, -38,
         3, 238, -228, -239, 178, -180, -39, 265, -267, 6, -9, -293, 291, -292, 8, 83, -86, 116, -120, 27,
         -28, -121, 174, -177, 207, -211, 105, -106, -212, 282, -284, 196, -197, -285, 15, 17, -18, 277, -278,
         59, 92, -95, 9, 80, 183, -186, 60, -61, 28, 106, 86, 171, 177, 280, -281, 262, 18, 12, 95, 38, 186,
         120, 89, 149, -150, 197, 278, 283, -287, -288, 301, -302, 211, 123, 180, 109, 214, 267, 284, 134,
         287, 225, 240, -241, 200, 281,),
        (),
        (),
        (162, 71, 61, 150, -72,),
        (241, -303,),
        (146, 292,),
        (253, 237,),
        (),
        (166, 257, 306, -308, 302,),
        (),
        (),
    ),
    (2, 3): (
        (-310, -2, -79, -170, -261, -11, -88, -179, -266, -47, -132, -223, -290, -309, -1, -4, 310, 2, 79,
         170, -78, -81, 261, 11, 88, 179, 266, 47, 132, 223, 290, 311, 3, 8, -172, 80, 85, 176, -263, 171,
         309, -311, 17, -169, 262, -13, 1, -3, 94, -260, 12, -90, 185, -10, 59, 5, -8, -181, 89, 148, 38, 239,
         -87, 180, -268, 267, 9, 292, -52, 14, -17, -137, 86, 120, 28, 58, -59, -228, 177, 211, 106, -178,
         -293, 284, 197, 6, -9, 78, -80, -265, -96, 18, 278, 27, -28, -48, 105, -106, 95, 83, -86, 186, 169,
         -171, -187, 174, -177, 61, 260, -262, -270, 15, -18, 10, -12, 92, -95, 35, -38, -39, 183, -186, 116,
         -120, -121, 87, -89, 281, 196, -197, 277, -278, 207, -211, -212, 117, -123, -124, 178, -180, 150,
         108, -109, 208, -214, -215, 287, 265, 302, -267, 282, -284, -285, 133, -134, 283, -287, -288, 224,
         -225, 199, -200, 280, -281,),
        (),
        (60, 161, 241, 149, -157, -162, -61, -150,),
        (240, -248, -241,),
        (291, 145, -146, -292,),
        (236, 252, -253, -237,),
        (72,),
        (),
        (160, -166, 251, -257, 301, -302,),
        (308,),
        (),
    ),
}


def kernel(panels, root_hbm, inverse_hbm, hamilton_hbm, margin_hbm, hamilton_mask_hbm,
           root_out, inverse_out, lowdin_out,
           root, inverse, hamilton, poly, margin, next_rows, root_in, inverse_in, hamilton_in,
           margin_in, hamilton_mask_in, load_sem, send_sem, recv_sem):
    cannon, rep = lax.axis_index("cannon"), lax.axis_index("rep")
    refs = {"R": root, "I": inverse, "H": hamilton, "P": poly, "M": margin}
    ahead, behind = lax.rem(cannon + 1, panels), lax.rem(cannon + panels - 1, panels)
    sibling, across = rep + 1 - 2 * lax.rem(rep, 2), lax.rem(rep + 2, 4)

    place = lax.rem(cannon, Z_PANELS)
    far = ((place == Z_PANELS - 1) & (rep >= 2)) | ((place == 0) & (rep < 2))
    beyond = lax.rem(cannon + jnp.where(place == 0, panels - 1, 1), panels)

    loads = [pltpu.make_async_copy(source, target, load_sem.at[n]) for n, (source, target) in enumerate((
        (margin_hbm, margin_in), (root_hbm, root_in), (inverse_hbm, inverse_in),
        (hamilton_mask_hbm, hamilton_mask_in), (hamilton_hbm, hamilton_in),
    ))]
    for load in loads:
        load.start()

    barrier = pltpu.get_barrier_semaphore()
    for peer in ((ahead, rep), (behind, rep), (cannon, sibling), (cannon, across)):
        pl.semaphore_signal(barrier, inc=1, device_id=peer, device_id_type=MESH)

    @pl.when(far)
    def _():
        pl.semaphore_signal(barrier, inc=1, device_id=(beyond, across), device_id_type=MESH)

    for array in (root, inverse, hamilton, poly):
        for row in range(SPAN):
            right = row + HALF
            if right < SPAN:
                array[row * BLK:(row + 1) * BLK, right * BLK:] = jnp.zeros((BLK, (SPAN - right) * BLK), jnp.bfloat16)
            left = row - HALF
            if left > 0:
                array[row * BLK:(row + 1) * BLK, :left * BLK] = jnp.zeros((BLK, left * BLK), jnp.bfloat16)

    for load in loads:
        load.wait()
    for array, source, scale in (
        (root, root_in, margin_in), (inverse, inverse_in, margin_in), (hamilton, hamilton_in, hamilton_mask_in),
    ):
        for j in range(ROWS):
            for b in range(2):
                keep = scale[b, j].astype(jnp.float32).astype(jnp.bfloat16)
                at = pl.multiple_of((j + 2 * rep + b) * BLK, BLK)
                array[pl.ds((j + HALF) * BLK, BLK), pl.ds(at, BLK)] = source[j, b] * keep
    for j in range(ROWS):
        for b in range(2):
            keep = margin_in[b, j].astype(jnp.float32)
            margin[pl.ds(rep * 8 + j * 2 + b, 1), :] = jnp.full((1, BLK), keep, jnp.float32)
    @pl.when(far)
    def _():
        pl.semaphore_wait(barrier, 5)

    @pl.when(jnp.logical_not(far))
    def _():
        pl.semaphore_wait(barrier, 4)

    def by_role(plan):
        for kind in KINDS:
            here = {PLAIN: (place > 0) & (place < Z_PANELS - 1), LAST: place == Z_PANELS - 1, FIRST: place == 0}[kind]
            for role in EVERY:
                @pl.when(here & (rep == role))
                def _():
                    plan(Role(kind, role, refs, send_sem, recv_sem, cannon, panels))


    def mask_row(i):
        return jnp.concatenate([margin[(t // 2) * 8 + i * 2 + t % 2:(t // 2) * 8 + i * 2 + t % 2 + 1, :]
                                for t in range(NS)], axis=1)

    def window(i):
        return slice(i * BLK, (i + NS) * BLK)

    def own(i):
        return slice((i + HALF) * BLK, (i + HALF + 1) * BLK)

    at_row = lax.broadcasted_iota(jnp.int32, (BLK, NS * BLK), 0)
    at_col = lax.broadcasted_iota(jnp.int32, (BLK, NS * BLK), 1)
    for i in range(ROWS):
        by_role(lambda d: d.play(i))
        product = jnp.dot(inverse[own(i), window(i)], root[window(i), window(i)], preferred_element_type=jnp.float32)
        diagonal = jnp.where(at_col - HALF * BLK == at_row, 1.5, 0.0).astype(jnp.float32)
        poly[own(i), window(i)] = (diagonal - 0.5 * (product * mask_row(i))).astype(jnp.bfloat16)

    for i in range(ROWS):
        by_role(lambda d: d.play(ROWS + i))
        product = jnp.dot(poly[own(i), window(i)], inverse[window(i), window(i)], preferred_element_type=jnp.float32)
        next_rows[i] = (product * mask_row(i)).astype(jnp.bfloat16)
        mine = next_rows[i, :, pl.ds(pl.multiple_of(2 * rep * BLK, 2 * BLK), 2 * BLK)]
        for b in range(2):
            inverse_out[i, b] = mine[:, b * BLK:(b + 1) * BLK]

    def narrow(first, second, i):
        cols = pl.ds(pl.multiple_of((i + 2 * rep) * BLK, BLK), 2 * BLK)
        return jnp.dot(first, second[window(i), cols], preferred_element_type=jnp.float32)

    by_role(lambda d: d.play(2 * ROWS))
    for i in range(ROWS):
        product = narrow(next_rows[i], hamilton, i)
        for b in range(2):
            keep = hamilton_mask_in[b, i].astype(jnp.float32)
            lowdin_out[i, b] = (product[:, b * BLK:(b + 1) * BLK] * keep).astype(jnp.bfloat16)

    by_role(lambda d: d.play(2 * ROWS + 1))
    for i in range(ROWS):
        product = narrow(root[own(i), window(i)], poly, i)
        for b in range(2):
            keep = margin_in[b, i].astype(jnp.float32)
            root_out[i, b] = (product[:, b * BLK:(b + 1) * BLK] * keep).astype(jnp.bfloat16)

    def finish(d):
        d.play(2 * ROWS + 2)
        d.drain()

    by_role(finish)


def store(*refs):
    held, arrived, left = refs[6:9], refs[9], refs[10]
    inward = [pltpu.make_async_copy(refs[n], held[n], arrived.at[n]) for n in range(3)]
    outward = [pltpu.make_async_copy(held[n], refs[3 + n], left.at[n]) for n in range(3)]
    for copy in inward:
        copy.start()
    for n in range(3):
        inward[n].wait()
        outward[n].start()
    for copy in outward:
        copy.wait()


def solution(mesh):
    panels = mesh.shape["cannon"]
    count = len(TABLE.rows)
    vmem = pl.BlockSpec(memory_space=pltpu.VMEM)

    def body(root_margin, inverse_root, hamiltonian, margin_mask, hamilton_mask):
        shape = jax.ShapeDtypeStruct(root_margin.shape, jnp.bfloat16)

        def run(*refs):
            kernel(panels, *refs)

        raw = pltpu.VMEM(root_margin.shape, jnp.bfloat16)
        band = pltpu.VMEM((SPAN * BLK, SPAN * BLK), jnp.bfloat16)
        results = pl.pallas_call(
            run,
            out_shape=(shape, shape, shape),
            in_specs=[pl.BlockSpec(memory_space=pltpu.HBM)] * 5,
            out_specs=(vmem, vmem, vmem),
            scratch_shapes=[
                band, band, band, band,
                pltpu.VMEM((4 * 8, BLK), jnp.float32),
                pltpu.VMEM((ROWS, BLK, NS * BLK), jnp.bfloat16),
                raw, raw, raw,
                pltpu.SMEM((2, ROWS), jnp.int32),
                pltpu.SMEM((2, ROWS), jnp.int32),
                pltpu.SemaphoreType.DMA((5,)),
                pltpu.SemaphoreType.DMA((count,)),
                pltpu.SemaphoreType.DMA((count,)),
            ],
            compiler_params=pltpu.CompilerParams(
                collective_id=0, has_side_effects=True, vmem_limit_bytes=60 << 20
            ),
            cost_estimate=pl.CostEstimate(flops=4 * 4 * 268435456, bytes_accessed=6 * 262144, transcendentals=0),
            name="newton_step",
        )(root_margin, inverse_root, hamiltonian, margin_mask.T, hamilton_mask.T)
        there = pl.BlockSpec(memory_space=pl.ANY)
        return pl.pallas_call(
            store,
            out_shape=(shape, shape, shape),
            in_specs=[there] * 3,
            out_specs=(there,) * 3,
            scratch_shapes=[raw, raw, raw, pltpu.SemaphoreType.DMA((3,)), pltpu.SemaphoreType.DMA((3,))],
            compiler_params=pltpu.CompilerParams(vmem_limit_bytes=60 << 20),
            name="store",
        )(*results)

    spec = P("cannon", "rep", None, None)
    mask = P("cannon", "rep")
    return jax.shard_map(body, mesh=mesh, in_specs=(spec, spec, spec, mask, mask),
                         out_specs=(spec, spec, spec), check_vma=False)
```
